512 devices in a mesh: series: 32 (over z, x_lo), tick: 16 (over y, x_hi, core).
Axes of the slice: x: 4 (x_hi: 2, x_lo: 2; x = x_hi * 2 + x_lo), y: 4, z: 16, core: 2. Of those that a mesh axis runs over, the one named last changes fastest.
Arguments:
- series_values: float32 [65536, 2048], P('series', 'tick'), may hold values from -8 to 8
- previous_sparse: float32 [65536, 2048], P('series', 'tick'), may hold values from -6 to 6
- row_picks: int32 [2048], replicated, may hold values from 0 to 65535, as said below
- tick_picks: int32 [512], replicated, may hold values from 0 to 2047, as said below
- sketch: float32 [512, 64], replicated, may hold values from -0.25 to 0.25
- thresholds: float32 [2048], P('tick'), may hold values from 0.3 to 3
Outputs:
- low_rank: float32 [65536, 2048], P('series', 'tick')
- sparse: float32 [65536, 2048], P('series', 'tick')
The draws below stay inside these ranges and needn't reach their ends.
Inputs may be any that keep to these rules, and one draw needn't show every extreme that they name: `row_picks`: 2048 distinct series; each aligned block of 2048 series holds at most 256 of them, and one block holds exactly 256. `tick_picks`: 512 distinct ticks.
All inputs are finite; a program needn't handle non-finite values.
Results may differ from the reference program's by a relative error of at most 0.0003.
Values sent between devices are 32-bit elements; how exact they have to be, the bound alone decides.
A program may use at most 64 MiB of HBM per device.

```python
import math
import jax
import jax.numpy as jnp
from jax import lax

ROWS_DEV = 2048
RANK = 64
SERIES = 65536
TICKS = 2048
SAMPLED_ROWS = 2048
SAMPLED_COLS = 512
CAP = 256


def draw_previous_sparse(key, part):
    key = jax.random.fold_in(key, 5)
    values = 2.0 * jnp.clip(jax.random.normal(key, (SERIES, TICKS), jnp.float32), -4.0, 4.0)
    return jnp.sign(values) * jnp.maximum(jnp.abs(values) - 2.0, 0.0)


def draw_row_picks(key, part):
    key = jax.random.fold_in(key, 11)
    key_busy, key_perm, key_level, key_noise, key_order = jax.random.split(key, 5)
    blocks = SERIES // ROWS_DEV
    busy = jax.random.randint(key_busy, (), 0, blocks)
    block_keys = jax.random.split(key_perm, blocks)
    local_rows = jax.vmap(lambda single: jax.random.permutation(single, ROWS_DEV)[:CAP])(block_keys)
    global_rows = local_rows.astype(jnp.int32) + (jnp.arange(blocks, dtype=jnp.int32) * ROWS_DEV)[:, None]
    levels = jax.random.randint(key_level, (blocks,), 0, 4)
    noise = jax.random.randint(key_noise, (blocks, CAP), 0, 2 ** 14)
    position = jnp.arange(blocks * CAP, dtype=jnp.int32).reshape(blocks, CAP)
    scores = (noise + levels[:, None] * 2 ** 12) * (blocks * CAP) + position
    is_busy = jnp.arange(blocks, dtype=jnp.int32) == busy
    scores = jnp.where(is_busy[:, None], -1, scores).astype(jnp.int32)
    values_unused, picked = lax.top_k(scores.reshape(-1), SAMPLED_ROWS - CAP)
    others = global_rows.reshape(-1)[picked]
    busy_rows = jnp.take(global_rows, busy, axis=0)
    together = jnp.concatenate([busy_rows, others]).astype(jnp.int32)
    order = jax.random.permutation(key_order, SAMPLED_ROWS)
    return together[order].astype(jnp.int32)


def draw_tick_picks(key, part):
    key = jax.random.fold_in(key, 13)
    return jax.random.permutation(key, TICKS)[:SAMPLED_COLS].astype(jnp.int32)


def block_scale(key, dims, cuts, smallest, high):
    level = 1.0
    for dim, blocks in cuts:
        heights = jax.random.uniform(jax.random.fold_in(jax.random.fold_in(key, 6), dim), (blocks,), jnp.float32, smallest / len(cuts), high / len(cuts))
        level = level * jnp.repeat(jnp.exp(heights), dims[dim] // blocks).reshape((-1,) + (1,) * (len(dims) - 1 - dim))
    return level


def centred(key, dims, scale, reach, pieces=(), kind=jnp.bfloat16):
    gain = block_scale(key, dims, pieces, -0.22, 0.18) if pieces else 1.0
    entries = jax.random.normal(key, dims, jnp.float32) * scale * gain
    return jnp.minimum(jnp.maximum(entries, -reach), reach).astype(kind)


def setup_inputs(seed: int = 0) -> dict:
    seeds = jax.random.split(jax.random.key(seed), 7)
    series_values = centred(seeds[0], (SERIES, TICKS), 1.0, 8.0, ((0, 32), (1, 16)), jnp.float32)
    previous_sparse = draw_previous_sparse(jax.random.fold_in(seeds[6], 71), 0)
    row_picks = draw_row_picks(jax.random.fold_in(seeds[6], 71), 0)
    tick_picks = draw_tick_picks(jax.random.fold_in(seeds[6], 71), 0)
    sketch = centred(seeds[4], (SAMPLED_COLS, RANK), SAMPLED_COLS ** -0.5, 0.25, (), jnp.float32)
    thresholds = jnp.clip(jnp.exp(math.log(3.0) - 2.3025851 * jax.random.uniform(seeds[5], (TICKS,), jnp.float32) ** block_scale(seeds[5], (TICKS,), ((0, 16),), -0.2, 0.2)), 0.3, 3.0)
    return {"series_values": series_values, "previous_sparse": previous_sparse, "row_picks": row_picks, "tick_picks": tick_picks, "sketch": sketch, "thresholds": thresholds}


def reference(series_values, previous_sparse, row_picks, tick_picks, sketch, thresholds):
    highest = lax.Precision.HIGHEST
    row_block = series_values[row_picks] - previous_sparse[row_picks]
    col_block = series_values[:, tick_picks] - previous_sparse[:, tick_picks]
    crossing = row_block[:, tick_picks]
    sketched = jnp.dot(crossing, sketch, precision=highest)
    right_factor = jnp.dot(sketched.T, row_block, precision=highest)
    core_block = right_factor[:, tick_picks]
    gram_matrix = jnp.dot(core_block, core_block.T, precision=highest)
    factor = jnp.linalg.cholesky(gram_matrix)
    panel_sum = jnp.dot(core_block, col_block.T, precision=highest)
    left_trans = jax.scipy.linalg.cho_solve((factor, True), panel_sum)
    low_rank = jnp.dot(left_trans.T, right_factor, precision=highest)
    difference = series_values - low_rank
    sparse = jnp.sign(difference) * jnp.maximum(jnp.abs(difference) - thresholds[None, :], 0.0)
    return (low_rank, sparse)
```

```python
import jax
import jax.numpy as jnp
from jax import lax
from jax.experimental import pallas as pl
from jax.experimental.pallas import tpu as pltpu
from jax.sharding import PartitionSpec as P

CAP = 256
RANK = 64
ROWS = 2048
COLS = 128
PICKS = 512
NT = (((1,), (1,)), ((), ()))
TN = (((0,), (0,)), ((), ()))
HI = lax.Precision.HIGHEST
F32 = jnp.float32
BF16 = jnp.bfloat16


def dot(a, b, dims=(((1,), (0,)), ((), ()))):
    return lax.dot_general(a, b, dims, precision=HI, preferred_element_type=F32)


def dot16(a, b, dims=(((1,), (0,)), ((), ()))):
    return lax.dot_general(a, b, dims, preferred_element_type=F32)


def iota(shape, dim):
    return lax.broadcasted_iota(jnp.int32, shape, dim)


def one_hot_rows(picks, row_start):
    local = picks - row_start
    inside = (local >= 0) & (local < ROWS)
    flags = jnp.where(inside, 1.0, 0.0).astype(BF16)
    upto = (iota((128, 128), 0) <= iota((128, 128), 1)).astype(F32).astype(BF16)
    along = dot16(flags, upto)
    total = dot16(flags, jnp.ones((128, 128), BF16))
    before = (iota((16, 16), 1) < iota((16, 16), 0)).astype(F32).astype(BF16)
    ahead = dot16(before, total.astype(BF16))
    slot = jnp.where(inside, along + ahead - 1.0, -1.0)
    marked = jnp.where(inside, local + 1, 0).astype(F32)
    lines = iota((CAP, 128), 0).astype(F32)
    found = jnp.zeros((CAP, 128), F32)
    for i in range(16):
        found = found + jnp.where(slot[i : i + 1] == lines, marked[i : i + 1], 0.0)
    chosen = jnp.sum(found, axis=1, keepdims=True) - 1.0
    return (chosen.astype(jnp.int32) == iota((CAP, ROWS), 1)).astype(F32).astype(BF16)


def main_kernel(
    series_hbm, sparse_hbm, row_ref, tick_ref, sketch_ref, panel_ref, weight_ref,
    values, residual, sampled, sk_part, sk_in, sk_full, rf_part, rf_in, rf_group, rf_far, rf_full,
    other, mine, from_core, chips_in, g_part, g_core, g_half, g_in, g_full,
    in_sem, t1_s, t1_r, t2_s, t2_r, s1_s, s1_r, s2_s, s2_r, s3_s, s3_r,
    c_s, c_r, p1_s, p1_r, p2_s, p2_r, g_s, g_r, gc_s, gc_r,
):
    s = lax.axis_index("series")
    t = lax.axis_index("tick")
    member, group = lax.rem(s, 8), s // 8
    chip, core = t // 2, lax.rem(t, 2)

    def tick_peer(d):
        return lax.rem(t + d, 16)

    def near(d):
        return group * 8 + lax.rem(member + d, 8)

    def far(d):
        return lax.rem(group + d, 4) * 8 + member

    def chip_peer(d):
        return lax.rem(chip + d, 8)

    def send(src, dst, send_sem, recv_sem, device):
        copy = pltpu.make_async_remote_copy(
            src_ref=src, dst_ref=dst, send_sem=send_sem, recv_sem=recv_sem,
            device_id=device, device_id_type=pl.DeviceIdType.MESH,
        )
        copy.start()
        return copy

    barrier = pltpu.get_barrier_semaphore()
    peers = [(s, tick_peer(d)) for d in range(1, 16)]
    peers += [(near(d), t) for d in range(1, 8)] + [(far(d), t) for d in range(1, 4)]
    for peer in peers:
        pl.semaphore_signal(barrier, inc=1, device_id=peer, device_id_type=pl.DeviceIdType.MESH)
    load_values = pltpu.make_async_copy(series_hbm, values, in_sem.at[0])
    load_sparse = pltpu.make_async_copy(sparse_hbm, residual, in_sem.at[1])
    load_values.start()
    load_sparse.start()

    ticks = iota((COLS, 128), 0) + t * COLS
    hits = [(ticks == tick_ref[i : i + 1, :]).astype(F32) for i in range(PICKS // 128)]
    hits = jnp.concatenate(hits, axis=1)
    local_sketch = dot(hits, sketch_ref[...])
    picked = dot16(jnp.ones((8, PICKS), BF16), hits.astype(BF16), NT)[0:1]
    rows = one_hot_rows(row_ref[...], s * ROWS)

    load_values.wait()
    load_sparse.wait()
    res = values[...] - residual[...]
    residual[...] = res
    high = res.astype(BF16)
    rest = res - high.astype(F32)
    mid = rest.astype(BF16)
    low = (rest - mid.astype(F32)).astype(BF16)
    sampled[...] = dot16(rows, high) + (dot16(rows, mid) + dot16(rows, low))
    part = dot(local_sketch.T, sampled[...], NT)
    for h in range(2):
        sk_part[h * 8 : h * 8 + 8] = part[:, h * 128 : h * 128 + 128].reshape(8, 8, 128)

    pl.semaphore_wait(barrier, len(peers))
    copies = [
        send(sk_part.at[tick_peer(d)], sk_in.at[d], t1_s.at[d], t1_r.at[d], (s, tick_peer(d)))
        for d in range(1, 16)
    ]
    total = sk_part[t]
    for copy in copies:
        copy.wait()
    for d in range(1, 16):
        total = total + sk_in[d]
    sk_full[t] = total
    copies = [
        send(sk_full.at[t], sk_full.at[t], t2_s.at[d], t2_r.at[d], (s, tick_peer(d)))
        for d in range(1, 16)
    ]
    for copy in copies:
        copy.wait()

    part = dot(sk_full[0:8].reshape(RANK, 128), sampled[0:128, :])
    part = part + dot(sk_full[8:16].reshape(RANK, 128), sampled[128:256, :])
    rf_part[...] = part.reshape(8, 8, COLS)
    copies = [
        send(rf_part.at[lax.rem(member + d, 8)], rf_in.at[d], s1_s.at[d], s1_r.at[d], (near(d), t))
        for d in range(1, 8)
    ]
    total = rf_part[member]
    for copy in copies:
        copy.wait()
    for d in range(1, 8):
        total = total + rf_in[d]
    rf_group[...] = total
    copies = [
        send(rf_group, rf_far.at[d], s2_s.at[d], s2_r.at[d], (far(d), t)) for d in range(1, 4)
    ]
    for copy in copies:
        copy.wait()
    for d in range(1, 4):
        total = total + rf_far[d]
    rf_full[member] = total
    copies = [
        send(rf_full.at[member], rf_full.at[member], s3_s.at[d], s3_r.at[d], (near(d), t))
        for d in range(1, 8)
    ]
    for copy in copies:
        copy.wait()

    right = rf_full[...].reshape(RANK, COLS)
    masked = right * picked
    gram = dot(masked, right, NT)
    g_part[...] = jnp.concatenate([gram[0:32], gram[32:64]], axis=1).reshape(2, 16, 128)
    sibling = (s, t + 1 - 2 * core)
    gram_copy = send(g_part.at[1 - core], g_core, gc_s.at[0], gc_r.at[0], sibling)
    panel_copies = []
    for c in range(8):
        start = pl.multiple_of((2 * c + 1 - core) * 128, 128)
        other[c] = dot(masked, residual[pl.ds(start, 128), :], NT)
        panel_copies.append(send(other.at[c], from_core.at[c], c_s.at[c], c_r.at[c], sibling))
    for c in range(8):
        start = pl.multiple_of((2 * c + core) * 128, 128)
        mine[c] = dot(masked, residual[pl.ds(start, 128), :], NT)
    gram_copy.wait()
    g_half[...] = g_part[core] + g_core[...]
    gram_copies = [
        send(g_half, g_in.at[d], g_s.at[d], g_r.at[d], (s, chip_peer(d) * 2 + core))
        for d in range(1, 8)
    ]
    for copy in panel_copies:
        copy.wait()
    mine[...] = mine[...] + from_core[...]

    copies = [
        send(
            mine.at[chip_peer(d)], chips_in.at[d], p1_s.at[d], p1_r.at[d],
            (s, chip_peer(d) * 2 + core),
        )
        for d in range(1, 8)
    ]
    for copy in gram_copies:
        copy.wait()
    total = g_half[...]
    for d in range(1, 8):
        total = total + g_in[d]
    g_full[core] = total
    gram_copy = send(g_full.at[core], g_full.at[core], gc_s.at[1], gc_r.at[1], sibling)
    for copy in copies:
        copy.wait()
    total = mine[chip]
    for d in range(1, 8):
        total = total + chips_in[d]
    panel_ref[t] = total
    copies = [
        send(panel_ref.at[t], panel_ref.at[t], p2_s.at[d], p2_r.at[d], (s, tick_peer(d)))
        for d in range(1, 16)
    ]

    gram_copy.wait()
    packed = g_full[...].reshape(32, 128)
    a = jnp.concatenate([packed[:, 0:64], packed[:, 64:128]], axis=0)
    x = right
    lines = iota((RANK, 1), 0)
    for k in range(RANK):
        inverse = 1.0 / a[k : k + 1, k : k + 1]
        column = a[:, k : k + 1]
        row_a = a[k : k + 1, :] * inverse
        row_x = x[k : k + 1, :] * inverse
        a = jnp.where(lines == k, row_a, a - column * row_a)
        x = jnp.where(lines == k, row_x, x - column * row_x)
    weight_ref[...] = x
    for copy in copies:
        copy.wait()


def last_kernel(panel_ref, weight_ref, values_ref, thresholds_ref, low_ref, sparse_ref):
    weight = weight_ref[...]
    bound = thresholds_ref[...]
    for i in range(panel_ref.shape[0]):
        at = slice(i * 128, i * 128 + 128)
        low = dot(panel_ref[i], weight, TN)
        gap = values_ref[at, :] - low
        low_ref[at, :] = low
        sparse_ref[at, :] = gap - jnp.minimum(jnp.maximum(gap, -bound), bound)


def on_device(series_values, previous_sparse, row_picks, tick_picks, sketch, thresholds):
    vmem = pl.BlockSpec(memory_space=pltpu.VMEM)
    hbm = pl.BlockSpec(memory_space=pl.ANY)
    dma = pltpu.SemaphoreType.DMA
    panel, weight = pl.pallas_call(
        main_kernel,
        out_shape=(
            jax.ShapeDtypeStruct((16, RANK, 128), F32),
            jax.ShapeDtypeStruct((RANK, COLS), F32),
        ),
        in_specs=[hbm, hbm, vmem, vmem, vmem],
        out_specs=(vmem, vmem),
        scratch_shapes=[
            pltpu.VMEM((ROWS, COLS), F32),
            pltpu.VMEM((ROWS, COLS), F32),
            pltpu.VMEM((CAP, COLS), F32),
            pltpu.VMEM((16, 8, 128), F32),
            pltpu.VMEM((16, 8, 128), F32),
            pltpu.VMEM((16, 8, 128), F32),
            pltpu.VMEM((8, 8, COLS), F32),
            pltpu.VMEM((8, 8, COLS), F32),
            pltpu.VMEM((8, COLS), F32),
            pltpu.VMEM((4, 8, COLS), F32),
            pltpu.VMEM((8, 8, COLS), F32),
            pltpu.VMEM((8, RANK, 128), F32),
            pltpu.VMEM((8, RANK, 128), F32),
            pltpu.VMEM((8, RANK, 128), F32),
            pltpu.VMEM((8, RANK, 128), F32),
            pltpu.VMEM((2, 16, 128), F32),
            pltpu.VMEM((16, 128), F32),
            pltpu.VMEM((16, 128), F32),
            pltpu.VMEM((8, 16, 128), F32),
            pltpu.VMEM((2, 16, 128), F32),
            dma((2,)),
            dma((16,)), dma((16,)), dma((16,)), dma((16,)),
            dma((8,)), dma((8,)), dma((4,)), dma((4,)), dma((8,)), dma((8,)),
            dma((8,)), dma((8,)), dma((8,)), dma((8,)), dma((16,)), dma((16,)),
            dma((8,)), dma((8,)), dma((2,)), dma((2,)),
        ],
        compiler_params=pltpu.CompilerParams(
            collective_id=0, has_side_effects=True, vmem_limit_bytes=32 << 20
        ),
        name="cur_core",
    )(
        series_values,
        previous_sparse,
        row_picks.reshape(16, 128),
        tick_picks.reshape(PICKS // 128, 128),
        sketch,
    )
    steps = 4
    return pl.pallas_call(
        last_kernel,
        grid=(steps,),
        out_shape=(jax.ShapeDtypeStruct((ROWS, COLS), F32),) * 2,
        in_specs=[
            pl.BlockSpec((16 // steps, RANK, 128), lambda i: (i, 0, 0)),
            pl.BlockSpec((RANK, COLS), lambda i: (0, 0)),
            pl.BlockSpec((ROWS // steps, COLS), lambda i: (i, 0)),
            pl.BlockSpec((1, COLS), lambda i: (0, 0)),
        ],
        out_specs=(pl.BlockSpec((ROWS // steps, COLS), lambda i: (i, 0)),) * 2,
        compiler_params=pltpu.CompilerParams(vmem_limit_bytes=16 << 20),
        name="low_rank_and_sparse",
    )(panel, weight, series_values, thresholds.reshape(1, COLS))


def solution(mesh):
    placed = (P("series", "tick"), P("series", "tick"), P(), P(), P(), P("tick"))
    return jax.shard_map(
        on_device,
        mesh=mesh,
        in_specs=placed,
        out_specs=(P("series", "tick"), P("series", "tick")),
        check_vma=False,
    )
```

```python
import jax
import jax.numpy as jnp
from jax import lax
from jax.experimental import pallas as pl
from jax.experimental.pallas import tpu as pltpu
from jax.sharding import PartitionSpec as P

CAP = 256
RANK = 64
ROWS = 2048
COLS = 128
PICKS = 512
HALF = ROWS // 2
NN = (((1,), (0,)), ((), ()))
NT = (((1,), (1,)), ((), ()))
F32 = jnp.float32
BF16 = jnp.bfloat16


def dot(a, b, dims=NN):
    return lax.dot_general(
        a, b, dims, precision=lax.Precision.HIGHEST, preferred_element_type=F32
    )


def dot16(a, b, dims=NN):
    return lax.dot_general(a, b, dims, preferred_element_type=F32)


def iota(shape, dim):
    return lax.broadcasted_iota(jnp.int32, shape, dim)


def split(x):
    high = x.astype(BF16)
    return high, (x - high.astype(F32)).astype(BF16)


def twice(x):
    zero = jnp.zeros_like(x)
    return jnp.concatenate(
        [jnp.concatenate([x, zero], axis=1), jnp.concatenate([zero, x], axis=1)], axis=0
    )


def find_rows(picks, row_start, slot_ref, mark_ref):
    local = picks - row_start
    inside = (local >= 0) & (local < ROWS)
    flags = jnp.where(inside, 1.0, 0.0).astype(BF16)
    upto = (iota((128, 128), 0) <= iota((128, 128), 1)).astype(F32).astype(BF16)
    along = dot16(flags, upto)
    total = dot16(flags, jnp.ones((128, 128), BF16))
    before = (iota((16, 16), 1) < iota((16, 16), 0)).astype(F32).astype(BF16)
    ahead = dot16(before, total.astype(BF16))
    slot_ref[...] = jnp.where(inside, along + ahead - 1.0, -1.0)
    mark_ref[...] = jnp.where(inside, local + 1, 0).astype(F32)
    lines = iota((CAP, 128), 0).astype(F32)

    def one(i, found):
        return found + jnp.where(slot_ref[pl.ds(i, 1), :] == lines, mark_ref[pl.ds(i, 1), :], 0.0)

    found = lax.fori_loop(0, 16, one, jnp.zeros((CAP, 128), F32))
    return (jnp.sum(found, axis=1, keepdims=True) - 1.0).astype(jnp.int32)


def solve(a, x):
    lines = iota((RANK, 1), 0)

    def round_of_8(_, state):
        a, x = state
        for k in range(8):
            inverse = 1.0 / a[k : k + 1, k : k + 1]
            column = a[:, k : k + 1]
            row_a = a[k : k + 1, :] * inverse
            row_x = x[k : k + 1, :] * inverse
            a = jnp.where(lines == k, row_a, a - column * row_a)
            x = jnp.where(lines == k, row_x, x - column * row_x)
        a = jnp.concatenate([a[8:], a[:8]], axis=0)
        x = jnp.concatenate([x[8:], x[:8]], axis=0)
        return pltpu.roll(a, 120, 1), x

    return lax.fori_loop(0, RANK // 8, round_of_8, (a, x))[1]


def main_kernel(
    series_hbm, sparse_hbm, row_hbm, tick_hbm, sketch_hbm, bound_hbm,
    panel_ref, weight_high, weight_low, bounds,
    values, previous, row_ref, tick_ref, sketch_ref, slot_ref, mark_ref, chosen_ref,
    res_high, res_low, sampled, sk_part, sk_core, sk_mine, sk_in, sk_full,
    rf_part, rf_in, rf_group, rf_far, rf_full,
    other, mine, from_core, chips_in, g_part, g_core, g_half, g_in, g_full,
    in_sem, t1_s, t1_r, t2_s, t2_r, s1_s, s1_r, s2_s, s2_r, s3_s, s3_r,
    c_s, c_r, p1_s, p1_r, p2_s, p2_r, g_s, g_r, gc_s, gc_r,
):
    s = lax.axis_index("series")
    t = lax.axis_index("tick")
    member, group = lax.rem(s, 8), s // 8
    chip, core = t // 2, lax.rem(t, 2)
    sibling = (s, t + 1 - 2 * core)

    def swap(g):
        return 4 * lax.rem((g + 1) // 2, 2)

    chunk = lax.rem(member + swap(group), 8)

    def near(d):
        return group * 8 + lax.rem(member + d, 8)

    def far(d):
        g = lax.rem(group + d, 4)
        return g * 8 + lax.rem(chunk + swap(g), 8)

    def chip_peer(d):
        return lax.rem(chip + d, 8)

    def send(src, dst, send_sem, recv_sem, device):
        copy = pltpu.make_async_remote_copy(
            src_ref=src, dst_ref=dst, send_sem=send_sem, recv_sem=recv_sem,
            device_id=device, device_id_type=pl.DeviceIdType.MESH,
        )
        copy.start()
        return copy

    barrier = pltpu.get_barrier_semaphore()

    def greet(device):
        pl.semaphore_signal(barrier, inc=1, device_id=device, device_id_type=pl.DeviceIdType.MESH)

    @pl.loop(1, 4)
    def _(d):
        greet((far(d), t))

    @pl.loop(1, 8)
    def _(d):
        greet((near(d), t))

    @pl.loop(1, 16)
    def _(d):
        greet((s, lax.rem(t + d, 16)))

    loads = []
    for i, (src, dst) in enumerate(
        [
            (row_hbm, row_ref), (tick_hbm, tick_ref), (sketch_hbm, sketch_ref),
            (series_hbm, values), (sparse_hbm, previous), (bound_hbm, bounds),
        ]
    ):
        load = pltpu.make_async_copy(src, dst, in_sem.at[i])
        load.start()
        loads.append(load)

    loads[0].wait()
    chosen = find_rows(row_ref[...], s * ROWS, slot_ref, mark_ref)
    chosen_ref[...] = jnp.broadcast_to(chosen, (CAP, 128))
    loads[1].wait()
    loads[2].wait()
    ticks = iota((COLS, 128), 0) + t * COLS
    hits = [(ticks == tick_ref[i : i + 1, :]).astype(F32) for i in range(PICKS // 128)]
    hits = jnp.concatenate(hits, axis=1).astype(BF16)
    picked = dot16(jnp.ones((8, PICKS), BF16), hits, NT)[0:1]
    first, second = split(sketch_ref[...])
    third = sketch_ref[...] - first.astype(F32) - second.astype(F32)
    pieces = dot16(jnp.concatenate([first, second, third.astype(BF16)], axis=0), hits, NT)
    local_sketch = pieces[0:64] + (pieces[64:128] + pieces[128:192])

    loads[3].wait()
    loads[4].wait()
    sampled[...] = jnp.zeros((CAP, COLS), F32)

    @pl.loop(0, ROWS // 256)
    def _(k):
        at = pl.ds(pl.multiple_of(k * 256, 256), 256)
        res = values[at, :] - previous[at, :]
        high, low = split(res)
        to = (
            pl.ds(pl.multiple_of(lax.rem(k, 4) * 256, 256), 256),
            pl.ds(pl.multiple_of(k // 4 * 128, 128), 128),
        )
        res_high[to] = high
        res_low[to] = low
        rest = (res - high.astype(F32) - low.astype(F32)).astype(BF16)
        line = iota((CAP, 128), 1) + k * 256
        rows = [(chosen_ref[...] == line + i * 128).astype(F32) for i in range(2)]
        rows = jnp.concatenate(rows, axis=1).astype(BF16)
        both = dot16(rows, jnp.concatenate([high, low], axis=1))
        sampled[...] += both[:, 0:128] + (both[:, 128:256] + dot16(rows, rest))

    part = dot(local_sketch, sampled[...], NT)
    for h in range(2):
        sk_part[h] = part[:, h * 128 : h * 128 + 128]
    loads[5].wait()

    pl.semaphore_wait(barrier, 25)
    copy = send(sk_part.at[1 - core], sk_core, t1_s.at[0], t1_r.at[0], sibling)
    copy.wait()
    sk_mine[...] = sk_part[core] + sk_core[...]
    copies = [
        send(sk_mine, sk_in.at[d], t2_s.at[d], t2_r.at[d], (s, chip_peer(d) * 2 + core))
        for d in range(1, 8)
    ]
    total = sk_mine[...]
    for d in range(1, 8):
        copies[d - 1].wait()
        total = total + sk_in[d]
    sk_full[core] = total
    copy = send(sk_full.at[core], sk_full.at[core], t1_s.at[1], t1_r.at[1], sibling)
    here = pl.ds(pl.multiple_of(core * 128, 128), 128)
    there = pl.ds(pl.multiple_of((1 - core) * 128, 128), 128)
    part = dot(total, sampled[here, :])
    copy.wait()

    part = part + dot(sk_full[1 - core], sampled[there, :])
    rf_part[...] = part.reshape(8, 8, COLS)
    copies = [
        send(
            rf_part.at[lax.rem(member + d + swap(group), 8)], rf_in.at[d], s1_s.at[d],
            s1_r.at[d], (near(d), t),
        )
        for d in range(1, 8)
    ]
    total = rf_part[chunk]
    for d in range(1, 8):
        copies[d - 1].wait()
        total = total + rf_in[d]
    rf_group[...] = total
    copies = [
        send(rf_group, rf_far.at[d], s2_s.at[d], s2_r.at[d], (far(d), t)) for d in range(1, 4)
    ]
    for d in range(1, 4):
        copies[d - 1].wait()
        total = total + rf_far[d]
    rf_full[chunk] = total
    copies = [
        send(rf_full.at[chunk], rf_full.at[chunk], s3_s.at[d], s3_r.at[d], (near(d), t))
        for d in range(1, 8)
    ]
    for copy in copies:
        copy.wait()

    right = rf_full[...].reshape(RANK, COLS)
    masked = right * picked
    gram = dot(masked, right, NT)
    g_part[...] = jnp.concatenate([gram[0:32], gram[32:64]], axis=1).reshape(2, 16, 128)
    gram_copy = send(g_part.at[1 - core], g_core, gc_s.at[0], gc_r.at[0], sibling)
    mask_high, mask_low = split(masked)
    mask_high, mask_low = twice(mask_high), twice(mask_low)

    def panel(half, dst):
        @pl.loop(0, 2)
        def _(i):
            at = pl.ds(pl.multiple_of(half * 512 + i * 256, 256), 256)
            high = res_high[at, :]
            value = dot16(high, mask_high, NT) + (
                dot16(high, mask_low, NT) + dot16(res_low[at, :], mask_high, NT)
            )
            dst[i] = value.reshape(4, 64, 128)

    panel(1 - core, other)
    panel_copies = [
        send(other.at[i], from_core.at[i], c_s.at[i], c_r.at[i], sibling) for i in range(2)
    ]
    gram_copy.wait()
    g_half[...] = g_part[core] + g_core[...]
    gram_copies = [
        send(g_half, g_in.at[d], g_s.at[d], g_r.at[d], (s, chip_peer(d) * 2 + core))
        for d in range(1, 8)
    ]
    panel(core, mine)

    for i in range(2):
        panel_copies[i].wait()
        mine[i] = mine[i] + from_core[i]
    copies = []
    for d in range(1, 8):
        peer = chip_peer(d)
        copies.append(
            send(
                mine.at[peer // 4, lax.rem(peer, 4)], chips_in.at[d], p1_s.at[d], p1_r.at[d],
                (s, peer * 2 + core),
            )
        )
    total = g_half[...]
    for d in range(1, 8):
        gram_copies[d - 1].wait()
        total = total + g_in[d]
    g_full[core] = total
    gram_copy = send(g_full.at[core], g_full.at[core], gc_s.at[1], gc_r.at[1], sibling)
    total = mine[chip // 4, lax.rem(chip, 4)]
    for d in range(1, 8):
        copies[d - 1].wait()
        total = total + chips_in[d]
    place = core * 8 + chip
    panel_ref[place] = total
    copies = [
        send(
            panel_ref.at[place], panel_ref.at[place], p2_s.at[d], p2_r.at[d],
            (s, lax.rem(t + d, 16)),
        )
        for d in range(1, 16)
    ]

    gram_copy.wait()
    packed = g_full[...].reshape(32, 128)
    zero = jnp.zeros((32, 64), F32)
    top = jnp.concatenate([packed[:, 0:64], zero], axis=1)
    low = jnp.concatenate([packed[:, 64:128], zero], axis=1)
    high, low = split(solve(jnp.concatenate([top, low], axis=0), right))
    weight_high[...] = twice(high)
    weight_low[...] = twice(low)
    for copy in copies:
        copy.wait()


def last_kernel(panel_ref, high_ref, low_ref, values_ref, bounds_ref, low_rank_ref, sparse_ref):
    high, low = split(panel_ref[...])
    weight = high_ref[...]
    both = dot16(high, weight) + (dot16(high, low_ref[...]) + dot16(low, weight))
    bound = bounds_ref[...]
    for i in range(2):
        low_rank = both[:, i * 128 : i * 128 + 128]
        gap = values_ref[i] - low_rank
        low_rank_ref[i] = low_rank
        sparse_ref[i] = gap - jnp.minimum(jnp.maximum(gap, -bound), bound)


def on_device(series_values, previous_sparse, row_picks, tick_picks, sketch, thresholds):
    vmem = pl.BlockSpec(memory_space=pltpu.VMEM)
    hbm = pl.BlockSpec(memory_space=pltpu.HBM)
    dma = pltpu.SemaphoreType.DMA
    panel, weight_high, weight_low, bounds = pl.pallas_call(
        main_kernel,
        out_shape=(
            jax.ShapeDtypeStruct((16, 64, 128), F32),
            jax.ShapeDtypeStruct((2 * RANK, 2 * COLS), BF16),
            jax.ShapeDtypeStruct((2 * RANK, 2 * COLS), BF16),
            jax.ShapeDtypeStruct((1, COLS), F32),
        ),
        in_specs=[hbm] * 6,
        out_specs=(vmem,) * 4,
        scratch_shapes=[
            pltpu.VMEM((ROWS, COLS), F32),
            pltpu.VMEM((ROWS, COLS), F32),
            pltpu.VMEM((16, 128), jnp.int32),
            pltpu.VMEM((PICKS // 128, 128), jnp.int32),
            pltpu.VMEM((RANK, PICKS), F32),
            pltpu.VMEM((16, 128), F32),
            pltpu.VMEM((16, 128), F32),
            pltpu.VMEM((CAP, 128), jnp.int32),
            pltpu.VMEM((HALF, 2 * COLS), BF16),
            pltpu.VMEM((HALF, 2 * COLS), BF16),
            pltpu.VMEM((CAP, COLS), F32),
            pltpu.VMEM((2, RANK, 128), F32),
            pltpu.VMEM((RANK, 128), F32),
            pltpu.VMEM((RANK, 128), F32),
            pltpu.VMEM((8, RANK, 128), F32),
            pltpu.VMEM((2, RANK, 128), F32),
            pltpu.VMEM((8, 8, COLS), F32),
            pltpu.VMEM((8, 8, COLS), F32),
            pltpu.VMEM((8, COLS), F32),
            pltpu.VMEM((4, 8, COLS), F32),
            pltpu.VMEM((8, 8, COLS), F32),
            pltpu.VMEM((2, 4, 64, 128), F32),
            pltpu.VMEM((2, 4, 64, 128), F32),
            pltpu.VMEM((2, 4, 64, 128), F32),
            pltpu.VMEM((8, 64, 128), F32),
            pltpu.VMEM((2, 16, 128), F32),
            pltpu.VMEM((16, 128), F32),
            pltpu.VMEM((16, 128), F32),
            pltpu.VMEM((8, 16, 128), F32),
            pltpu.VMEM((2, 16, 128), F32),
            dma((6,)),
            dma((2,)), dma((2,)), dma((8,)), dma((8,)),
            dma((8,)), dma((8,)), dma((4,)), dma((4,)), dma((8,)), dma((8,)),
            dma((2,)), dma((2,)), dma((8,)), dma((8,)), dma((16,)), dma((16,)),
            dma((8,)), dma((8,)), dma((2,)), dma((2,)),
        ],
        compiler_params=pltpu.CompilerParams(
            collective_id=0, has_side_effects=True, vmem_limit_bytes=53 << 20
        ),
        name="cur_core",
    )(
        series_values,
        previous_sparse,
        row_picks.reshape(16, 128),
        tick_picks.reshape(PICKS // 128, 128),
        sketch.T,
        thresholds.reshape(1, COLS),
    )
    steps = 4
    block = pl.BlockSpec((2, HALF // steps, COLS), lambda i: (0, i, 0))
    whole = pl.BlockSpec((2 * RANK, 2 * COLS), lambda i: (0, 0))
    low_rank, sparse = pl.pallas_call(
        last_kernel,
        grid=(steps,),
        out_shape=(jax.ShapeDtypeStruct((2, HALF, COLS), F32),) * 2,
        in_specs=[
            pl.BlockSpec((HALF // steps, 128), lambda i: (i, 0)),
            whole,
            whole,
            block,
            pl.BlockSpec((1, COLS), lambda i: (0, 0)),
        ],
        out_specs=(block, block),
        compiler_params=pltpu.CompilerParams(vmem_limit_bytes=16 << 20),
        name="low_rank_and_sparse",
    )(panel.reshape(HALF, 128), weight_high, weight_low, series_values.reshape(2, HALF, COLS), bounds)
    return low_rank.reshape(ROWS, COLS), sparse.reshape(ROWS, COLS)


def solution(mesh):
    placed = (P("series", "tick"), P("series", "tick"), P(), P(), P(), P("tick"))
    return jax.shard_map(
        on_device,
        mesh=mesh,
        in_specs=placed,
        out_specs=(P("series", "tick"), P("series", "tick")),
        check_vma=False,
    )
```

```python
import jax
import jax.numpy as jnp
from jax import lax
from jax.experimental import pallas as pl
from jax.experimental.pallas import tpu as pltpu
from jax.sharding import PartitionSpec as P

CAP = 256
RANK = 64
ROWS = 2048
COLS = 128
PICKS = 512
HALF = ROWS // 2
NN = (((1,), (0,)), ((), ()))
NT = (((1,), (1,)), ((), ()))
F32 = jnp.float32
BF16 = jnp.bfloat16


def dot(a, b, dims=NN):
    return lax.dot_general(
        a, b, dims, precision=lax.Precision.HIGHEST, preferred_element_type=F32
    )


def dot16(a, b, dims=NN):
    return lax.dot_general(
        a, b, dims, precision=lax.Precision.DEFAULT, preferred_element_type=F32
    )


def iota(shape, dim):
    return lax.broadcasted_iota(jnp.int32, shape, dim)


def split(x):
    high = x.astype(BF16)
    return high, (x - high.astype(F32)).astype(BF16)


def twice(x):
    zero = jnp.zeros_like(x)
    return jnp.concatenate(
        [jnp.concatenate([x, zero], axis=1), jnp.concatenate([zero, x], axis=1)], axis=0
    )


def find_rows(picks, row_start, slot_ref, mark_ref):
    local = picks - row_start
    inside = (local >= 0) & (local < ROWS)
    flags = jnp.where(inside, 1.0, 0.0).astype(BF16)
    upto = (iota((128, 128), 0) <= iota((128, 128), 1)).astype(F32).astype(BF16)
    along = dot16(flags, upto)
    total = dot16(flags, jnp.ones((128, 128), BF16))
    before = (iota((16, 16), 1) < iota((16, 16), 0)).astype(F32).astype(BF16)
    ahead = dot16(before, total.astype(BF16))
    slot_ref[...] = jnp.where(inside, along + ahead - 1.0, -1.0)
    mark_ref[...] = jnp.where(inside, local + 1, 0).astype(F32)
    lines = iota((CAP, 128), 0).astype(F32)

    def one(i, found):
        return found + jnp.where(slot_ref[pl.ds(i, 1), :] == lines, mark_ref[pl.ds(i, 1), :], 0.0)

    found = lax.fori_loop(0, 16, one, jnp.zeros((CAP, 128), F32))
    return (jnp.sum(found, axis=1, keepdims=True) - 1.0).astype(jnp.int32)


def solve(a, x):
    lines = iota((8, 128), 0)

    def round_of_8(_, state):
        a, x = state
        columns = [
            tuple(jnp.broadcast_to(part[:, k : k + 1], (part.shape[0], 128)) for part in a)
            for k in range(8)
        ]
        for k in range(8):
            top, rest = columns[k]
            inverse = 1.0 / top[k : k + 1, :]

            def eliminate(both, top=top, rest=rest, inverse=inverse, k=k):
                row = both[0][k : k + 1, :] * inverse
                return jnp.where(lines == k, row, both[0] - top * row), both[1] - rest * row

            columns = [c if i <= k else eliminate(c) for i, c in enumerate(columns)]
            a, x = eliminate(a), eliminate(x)
        a, x = (
            (both[1][0:8], jnp.concatenate([both[1][8:], both[0]], axis=0)) for both in (a, x)
        )
        return tuple(pltpu.roll(part, 120, 1) for part in a), x

    return jnp.concatenate(lax.fori_loop(0, RANK // 8, round_of_8, (a, x))[1], axis=0)


def main_kernel(
    series_hbm, sparse_hbm, row_hbm, tick_hbm, sketch_hbm, bound_hbm,
    panel_ref, weight_high, weight_low, bounds,
    values, previous, row_ref, tick_ref, sketch_ref, slot_ref, mark_ref, chosen_ref,
    res_high, res_low, sampled, sk_part, sk_core, sk_mine, sk_in, sib_rows,
    rf_part, rf_in, rf_group, rf_far, rf_full,
    other, mine, from_core, chips_in, g_part, g_core, g_half, g_in, g_full,
    in_sem, t1_s, t1_r, t2_s, t2_r, s1_s, s1_r, s2_s, s2_r, s3_s, s3_r,
    c_s, c_r, p1_s, p1_r, p2_s, p2_r, p3_s, p3_r, g_s, g_r, gc_s, gc_r,
):
    s = lax.axis_index("series")
    t = lax.axis_index("tick")
    member, group = lax.rem(s, 8), s // 8
    chip, core = t // 2, lax.rem(t, 2)
    sibling = (s, t + 1 - 2 * core)

    def swap(g):
        return 4 * lax.rem((g + 1) // 2, 2)

    chunk = lax.rem(member + swap(group), 8)

    def near(d):
        return group * 8 + lax.rem(member + d, 8)

    def far(d):
        g = lax.rem(group + d, 4)
        return g * 8 + lax.rem(chunk + swap(g), 8)

    def chip_peer(d):
        return lax.rem(chip + d, 8)

    def send(src, dst, send_sem, recv_sem, device):
        copy = pltpu.make_async_remote_copy(
            src_ref=src, dst_ref=dst, send_sem=send_sem, recv_sem=recv_sem,
            device_id=device, device_id_type=pl.DeviceIdType.MESH,
        )
        copy.start()
        return copy

    barrier = pltpu.get_barrier_semaphore()

    def greet(device):
        pl.semaphore_signal(barrier, inc=1, device_id=device, device_id_type=pl.DeviceIdType.MESH)

    loads = []
    for i, (src, dst) in enumerate(
        [
            (row_hbm, row_ref), (tick_hbm, tick_ref), (sketch_hbm, sketch_ref),
            (series_hbm, values), (sparse_hbm, previous), (bound_hbm, bounds),
        ]
    ):
        load = pltpu.make_async_copy(src, dst, in_sem.at[i])
        load.start()
        loads.append(load)

    @pl.loop(1, 4)
    def _(d):
        greet((far(d), t))

    @pl.loop(1, 8)
    def _(d):
        greet((near(d), t))
        greet((near(d), sibling[1]))

    @pl.loop(1, 16)
    def _(d):
        greet((s, lax.rem(t + d, 16)))

    loads[0].wait()
    chosen = find_rows(row_ref[...], s * ROWS, slot_ref, mark_ref)
    chosen_ref[...] = jnp.broadcast_to(chosen, (CAP, 128))
    loads[1].wait()
    loads[2].wait()
    ticks = iota((COLS, 128), 0) + t * COLS
    hits = [(ticks == tick_ref[i : i + 1, :]).astype(F32) for i in range(PICKS // 128)]
    hits = jnp.concatenate(hits, axis=1).astype(BF16)
    picked = dot16(jnp.ones((8, PICKS), BF16), hits, NT)[0:1]
    first, second = split(sketch_ref[...])
    third = sketch_ref[...] - first.astype(F32) - second.astype(F32)
    pieces = dot16(jnp.concatenate([first, second, third.astype(BF16)], axis=0), hits, NT)
    local_sketch = pieces[0:64] + (pieces[64:128] + pieces[128:192])

    loads[3].wait()
    loads[4].wait()
    sampled[...] = jnp.zeros((CAP, COLS), F32)

    @pl.loop(0, ROWS // 256, unroll=4)
    def _(k):
        at = pl.ds(pl.multiple_of(k * 256, 256), 256)
        res = values[at, :] - previous[at, :]
        high, low = split(res)
        to = (
            pl.ds(pl.multiple_of(lax.rem(k, 4) * 256, 256), 256),
            pl.ds(pl.multiple_of(k // 4 * 128, 128), 128),
        )
        res_high[to] = high
        res_low[to] = low
        rest = (res - high.astype(F32) - low.astype(F32)).astype(BF16)
        line = iota((CAP, 128), 1) + k * 256
        rows = [(chosen_ref[...] == line + i * 128).astype(F32) for i in range(2)]
        rows = jnp.concatenate(rows, axis=1).astype(BF16)
        both = dot16(rows, jnp.concatenate([high, low], axis=1))
        sampled[...] += both[:, 0:128] + (both[:, 128:256] + dot16(rows, rest))

    part = dot(local_sketch, sampled[...], NT)
    for h in range(2):
        sk_part[h] = part[:, h * 128 : h * 128 + 128]
    loads[5].wait()

    pl.semaphore_wait(barrier, 32)
    copy = send(sk_part.at[1 - core], sk_core, t1_s.at[0], t1_r.at[0], sibling)
    here = pl.ds(pl.multiple_of(core * 128, 128), 128)
    there = pl.ds(pl.multiple_of((1 - core) * 128, 128), 128)
    rows_copy = send(sampled.at[there, :], sib_rows, t1_s.at[1], t1_r.at[1], sibling)
    copy.wait()
    sk_mine[...] = sk_part[core] + sk_core[...]
    copies = [
        send(sk_mine, sk_in.at[d], t2_s.at[d], t2_r.at[d], (s, chip_peer(d) * 2 + core))
        for d in range(1, 8)
    ]
    total = sk_mine[...]
    for d in range(1, 8):
        copies[d - 1].wait()
        total = total + sk_in[d]
    rows_copy.wait()

    rf_part[1] = dot(total, sib_rows[...]).reshape(8, 8, COLS)
    copies = [
        send(
            rf_part.at[1, lax.rem(member + d + swap(group), 8)], rf_in.at[1, d],
            s1_s.at[1, d], s1_r.at[1, d], (near(d), sibling[1]),
        )
        for d in range(8)
    ]
    rf_part[0] = dot(total, sampled[here, :]).reshape(8, 8, COLS)
    copies += [
        send(
            rf_part.at[0, lax.rem(member + d + swap(group), 8)], rf_in.at[0, d],
            s1_s.at[0, d], s1_r.at[0, d], (near(d), t),
        )
        for d in range(1, 8)
    ]
    total = rf_part[0, chunk]
    for copy in copies:
        copy.wait()
    for d in range(1, 8):
        total = total + rf_in[0, d]
    for d in range(8):
        total = total + rf_in[1, d]
    rf_group[...] = total
    copies = [
        send(rf_group, rf_far.at[d], s2_s.at[d], s2_r.at[d], (far(d), t)) for d in range(1, 4)
    ]
    for d in range(1, 4):
        copies[d - 1].wait()
        total = total + rf_far[d]
    rf_full[chunk] = total
    copies = [
        send(rf_full.at[chunk], rf_full.at[chunk], s3_s.at[d], s3_r.at[d], (near(d), t))
        for d in range(1, 8)
    ]
    for copy in copies:
        copy.wait()

    right = rf_full[...].reshape(RANK, COLS)
    masked = right * picked
    gram = dot(masked, right, NT)
    g_part[...] = jnp.concatenate([gram[0:32], gram[32:64]], axis=1).reshape(2, 16, 128)
    gram_copy = send(g_part.at[1 - core], g_core, gc_s.at[0], gc_r.at[0], sibling)
    mask_high, mask_low = split(masked)
    mask_high, mask_low = twice(mask_high), twice(mask_low)

    def panel_piece(half, i):
        at = pl.ds(pl.multiple_of(half * 512 + i * 256, 256), 256)
        high = res_high[at, :]
        value = dot16(high, mask_high, NT) + (
            dot16(high, mask_low, NT) + dot16(res_low[at, :], mask_high, NT)
        )
        return value.reshape(8, 32, 128)

    panel_copies = []
    for i in range(2):
        other[i] = panel_piece(1 - core, i)
        panel_copies.append(send(other.at[i], from_core.at[i], c_s.at[i], c_r.at[i], sibling))
    gram_copy.wait()
    g_half[...] = g_part[core] + g_core[...]
    gram_copies = [
        send(g_half, g_in.at[d], g_s.at[d], g_r.at[d], (s, chip_peer(d) * 2 + core))
        for d in range(1, 8)
    ]

    chip_copies = []
    for i in range(2):
        own = panel_piece(core, i)
        panel_copies[i].wait()
        mine[i] = own + from_core[i]
        chip_copies.append(
            [
                send(
                    mine.at[i, chip_peer(d)], chips_in.at[i, d], p1_s.at[i, d], p1_r.at[i, d],
                    (s, chip_peer(d) * 2 + core),
                )
                for d in range(1, 8)
            ]
        )
    total = g_half[...]
    for d in range(1, 8):
        gram_copies[d - 1].wait()
        total = total + g_in[d]
    g_full[core] = total
    gram_copy = send(g_full.at[core], g_full.at[core], gc_s.at[1], gc_r.at[1], sibling)
    gathers, passes = [], []
    for i in range(2):
        total = mine[i, chip]
        for d in range(1, 8):
            chip_copies[i][d - 1].wait()
            total = total + chips_in[i, d]
        panel_ref[core, i, chip] = total
        place = panel_ref.at[core, i, chip]
        gathers.append(
            [
                send(place, place, p2_s.at[i, d], p2_r.at[i, d], (s, chip_peer(d) * 2 + core))
                for d in range(1, 8)
            ]
        )
        passes.append(send(place, place, p3_s.at[i, 0], p3_r.at[i, 0], sibling))

    gram_copy.wait()
    packed = g_full[...].reshape(32, 128)
    zero = jnp.zeros((32, 64), F32)
    top = jnp.concatenate([packed[:, 0:64], zero], axis=1)
    low = jnp.concatenate([packed[:, 64:128], zero], axis=1)
    solved = solve(
        (top[0:8], jnp.concatenate([top[8:], low], axis=0)), (right[0:8], right[8:])
    )
    high, low = split(solved)
    weight_high[...] = twice(high)
    weight_low[...] = twice(low)
    for i in range(2):
        for d in range(1, 8):
            gathers[i][d - 1].wait()
            place = panel_ref.at[core, i, chip_peer(8 - d)]
            passes.append(send(place, place, p3_s.at[i, d], p3_r.at[i, d], sibling))
    for copy in passes:
        copy.wait()


def last_kernel(panel_ref, high_ref, low_ref, values_ref, bounds_ref, low_rank_ref, sparse_ref):
    high, low = split(panel_ref[...])
    weight = high_ref[...]
    both = dot16(high, weight) + (dot16(high, low_ref[...]) + dot16(low, weight))
    bound = bounds_ref[...]
    for i in range(2):
        low_rank = both[:, i * 128 : i * 128 + 128]
        gap = values_ref[i] - low_rank
        low_rank_ref[i] = low_rank
        sparse_ref[i] = gap - jnp.minimum(jnp.maximum(gap, -bound), bound)


def on_device(series_values, previous_sparse, row_picks, tick_picks, sketch, thresholds):
    vmem = pl.BlockSpec(memory_space=pltpu.VMEM)
    hbm = pl.BlockSpec(memory_space=pltpu.HBM)
    dma = pltpu.SemaphoreType.DMA
    panel, weight_high, weight_low, bounds = pl.pallas_call(
        main_kernel,
        out_shape=(
            jax.ShapeDtypeStruct((2, 2, 8, 32, 128), F32),
            jax.ShapeDtypeStruct((2 * RANK, 2 * COLS), BF16),
            jax.ShapeDtypeStruct((2 * RANK, 2 * COLS), BF16),
            jax.ShapeDtypeStruct((1, COLS), F32),
        ),
        in_specs=[hbm] * 6,
        out_specs=(vmem,) * 4,
        scratch_shapes=[
            pltpu.VMEM((ROWS, COLS), F32),
            pltpu.VMEM((ROWS, COLS), F32),
            pltpu.VMEM((16, 128), jnp.int32),
            pltpu.VMEM((PICKS // 128, 128), jnp.int32),
            pltpu.VMEM((RANK, PICKS), F32),
            pltpu.VMEM((16, 128), F32),
            pltpu.VMEM((16, 128), F32),
            pltpu.VMEM((CAP, 128), jnp.int32),
            pltpu.VMEM((HALF, 2 * COLS), BF16),
            pltpu.VMEM((HALF, 2 * COLS), BF16),
            pltpu.VMEM((CAP, COLS), F32),
            pltpu.VMEM((2, RANK, 128), F32),
            pltpu.VMEM((RANK, 128), F32),
            pltpu.VMEM((RANK, 128), F32),
            pltpu.VMEM((8, RANK, 128), F32),
            pltpu.VMEM((128, COLS), F32),
            pltpu.VMEM((2, 8, 8, COLS), F32),
            pltpu.VMEM((2, 8, 8, COLS), F32),
            pltpu.VMEM((8, COLS), F32),
            pltpu.VMEM((4, 8, COLS), F32),
            pltpu.VMEM((8, 8, COLS), F32),
            pltpu.VMEM((2, 8, 32, 128), F32),
            pltpu.VMEM((2, 8, 32, 128), F32),
            pltpu.VMEM((2, 8, 32, 128), F32),
            pltpu.VMEM((2, 8, 32, 128), F32),
            pltpu.VMEM((2, 16, 128), F32),
            pltpu.VMEM((16, 128), F32),
            pltpu.VMEM((16, 128), F32),
            pltpu.VMEM((8, 16, 128), F32),
            pltpu.VMEM((2, 16, 128), F32),
            dma((6,)),
            dma((2,)), dma((2,)), dma((8,)), dma((8,)),
            dma((2, 8)), dma((2, 8)), dma((4,)), dma((4,)), dma((8,)), dma((8,)),
            dma((2,)), dma((2,)), dma((2, 8)), dma((2, 8)), dma((2, 8)), dma((2, 8)),
            dma((2, 8)), dma((2, 8)),
            dma((8,)), dma((8,)), dma((2,)), dma((2,)),
        ],
        compiler_params=pltpu.CompilerParams(
            collective_id=0, has_side_effects=True, vmem_limit_bytes=24 << 20
        ),
        name="cur_core",
    )(
        *(
            pltpu.with_memory_space_constraint(x, pltpu.HBM)
            for x in (
                series_values,
                previous_sparse,
                row_picks.reshape(16, 128),
                tick_picks.reshape(PICKS // 128, 128),
                sketch.T,
                thresholds.reshape(1, COLS),
            )
        )
    )
    steps = 2
    block = pl.BlockSpec((2, HALF // steps, COLS), lambda i: (0, i, 0))
    whole = pl.BlockSpec((2 * RANK, 2 * COLS), lambda i: (0, 0))
    low_rank, sparse = pl.pallas_call(
        last_kernel,
        grid=(steps,),
        out_shape=(jax.ShapeDtypeStruct((2, HALF, COLS), F32),) * 2,
        in_specs=[
            pl.BlockSpec((HALF // steps, 128), lambda i: (i, 0)),
            whole,
            whole,
            block,
            pl.BlockSpec((1, COLS), lambda i: (0, 0)),
        ],
        out_specs=(block, block),
        compiler_params=pltpu.CompilerParams(vmem_limit_bytes=16 << 20),
        name="low_rank_and_sparse",
    )(panel.reshape(HALF, 128), weight_high, weight_low, series_values.reshape(2, HALF, COLS), bounds)
    return low_rank.reshape(ROWS, COLS), sparse.reshape(ROWS, COLS)


def solution(mesh):
    placed = (P("series", "tick"), P("series", "tick"), P(), P(), P(), P("tick"))
    return jax.shard_map(
        on_device,
        mesh=mesh,
        in_specs=placed,
        out_specs=(P("series", "tick"), P("series", "tick")),
        check_vma=False,
    )
```

```python
import jax
import jax.numpy as jnp
from jax import lax
from jax.experimental import pallas as pl
from jax.experimental.pallas import tpu as pltpu
from jax.sharding import PartitionSpec as P

CAP = 256
RANK = 64
ROWS = 2048
COLS = 128
PICKS = 512
HALF = ROWS // 2
NN = (((1,), (0,)), ((), ()))
NT = (((1,), (1,)), ((), ()))
F32 = jnp.float32
BF16 = jnp.bfloat16


def dot(a, b, dims=NN):
    return lax.dot_general(
        a, b, dims, precision=lax.Precision.HIGHEST, preferred_element_type=F32
    )


def dot16(a, b, dims=NN):
    return lax.dot_general(
        a, b, dims, precision=lax.Precision.DEFAULT, preferred_element_type=F32
    )


def iota(shape, dim):
    return lax.broadcasted_iota(jnp.int32, shape, dim)


def split(x):
    high = x.astype(BF16)
    return high, (x - high.astype(F32)).astype(BF16)


def twice(x):
    zero = jnp.zeros_like(x)
    return jnp.concatenate(
        [jnp.concatenate([x, zero], axis=1), jnp.concatenate([zero, x], axis=1)], axis=0
    )


def find_rows(picks, row_start, slot_ref, mark_ref):
    local = picks - row_start
    inside = (local >= 0) & (local < ROWS)
    flags = jnp.where(inside, 1.0, 0.0).astype(BF16)
    upto = (iota((128, 128), 0) <= iota((128, 128), 1)).astype(F32).astype(BF16)
    along = dot16(flags, upto)
    total = dot16(flags, jnp.ones((128, 128), BF16))
    before = (iota((16, 16), 1) < iota((16, 16), 0)).astype(F32).astype(BF16)
    ahead = dot16(before, total.astype(BF16))
    slot_ref[...] = jnp.where(inside, along + ahead - 1.0, -1.0)
    mark_ref[...] = jnp.where(inside, local + 1, 0).astype(F32)
    lines = iota((CAP, 128), 0).astype(F32)

    def one(i, found):
        return found + jnp.where(slot_ref[pl.ds(i, 1), :] == lines, mark_ref[pl.ds(i, 1), :], 0.0)

    found = lax.fori_loop(0, 16, one, jnp.zeros((CAP, 128), F32))
    return (jnp.sum(found, axis=1, keepdims=True) - 1.0).astype(jnp.int32)


def solve(a, x):
    lines = iota((8, 128), 0)

    def round_of_8(_, state):
        a, x = state
        columns = [
            tuple(jnp.broadcast_to(part[:, k : k + 1], (part.shape[0], 128)) for part in a)
            for k in range(8)
        ]
        for k in range(8):
            top, rest = columns[k]
            inverse = 1.0 / top[k : k + 1, :]

            def eliminate(both, top=top, rest=rest, inverse=inverse, k=k):
                row = both[0][k : k + 1, :] * inverse
                return jnp.where(lines == k, row, both[0] - top * row), both[1] - rest * row

            columns = [c if i <= k else eliminate(c) for i, c in enumerate(columns)]
            a, x = eliminate(a), eliminate(x)
        a, x = (
            (both[1][0:8], jnp.concatenate([both[1][8:], both[0]], axis=0)) for both in (a, x)
        )
        return tuple(pltpu.roll(part, 120, 1) for part in a), x

    return jnp.concatenate(lax.fori_loop(0, RANK // 8, round_of_8, (a, x))[1], axis=0)


def main_kernel(
    series_hbm, sparse_hbm, row_hbm, tick_hbm, sketch_hbm, bound_hbm,
    low_ref, values, bounds,
    previous, row_ref, tick_ref, sketch_ref, slot_ref, mark_ref, chosen_ref,
    res_high, res_low, sampled, sk_part, sk_core, sk_mine, sk_in, sib_rows,
    rf_part, rf_in, rf_group, rf_far, rf_full,
    other, mine, from_core, chips_in, panel, g_part, g_core, g_half, g_in, g_full,
    in_sem, t1_s, t1_r, t2_s, t2_r, s1_s, s1_r, s2_s, s2_r, s3_s, s3_r,
    c_s, c_r, p1_s, p1_r, p2_s, p2_r, p3_s, p3_r, g_s, g_r, gc_s, gc_r,
):
    s = lax.axis_index("series")
    t = lax.axis_index("tick")
    member, group = lax.rem(s, 8), s // 8
    chip, core = t // 2, lax.rem(t, 2)
    sibling = (s, t + 1 - 2 * core)

    def swap(g):
        return 4 * (g // 2)

    chunk = lax.rem(member + swap(group), 8)

    def near(d):
        return group * 8 + lax.rem(member + d, 8)

    def far(d):
        g = lax.rem(group + d, 4)
        return g * 8 + lax.rem(chunk + swap(g), 8)

    def chip_peer(d):
        return lax.rem(chip + d, 8)

    def send(src, dst, send_sem, recv_sem, device):
        copy = pltpu.make_async_remote_copy(
            src_ref=src, dst_ref=dst, send_sem=send_sem, recv_sem=recv_sem,
            device_id=device, device_id_type=pl.DeviceIdType.MESH,
        )
        copy.start()
        sent.append(copy)
        return copy

    sent = []

    def settle(keep=0):
        while len(sent) > keep:
            sent.pop(0).wait_send()

    barrier = pltpu.get_barrier_semaphore()

    def greet(device):
        pl.semaphore_signal(barrier, inc=1, device_id=device, device_id_type=pl.DeviceIdType.MESH)

    loads = []
    for i, (src, dst) in enumerate(
        [
            (row_hbm, row_ref), (tick_hbm, tick_ref), (sketch_hbm, sketch_ref),
            (series_hbm.at[0:HALF], values.at[0:HALF]),
            (sparse_hbm.at[0:HALF], previous.at[0:HALF]),
            (series_hbm.at[HALF:ROWS], values.at[HALF:ROWS]),
            (sparse_hbm.at[HALF:ROWS], previous.at[HALF:ROWS]),
            (bound_hbm, bounds),
        ]
    ):
        load = pltpu.make_async_copy(src, dst, in_sem.at[i])
        load.start()
        loads.append(load)

    for d in range(1, 16):
        greet((s, lax.rem(t + d, 16)))
    for d in range(1, 8):
        greet((near(d), t))
        greet((near(d), sibling[1]))
    for d in range(1, 4):
        greet((far(d), t))

    loads[0].wait()
    chosen = find_rows(row_ref[...], s * ROWS, slot_ref, mark_ref)
    chosen_ref[...] = jnp.broadcast_to(chosen, (CAP, 128))
    loads[1].wait()
    loads[2].wait()
    ticks = iota((COLS, 128), 0) + t * COLS
    hits = [(ticks == tick_ref[i : i + 1, :]).astype(F32) for i in range(PICKS // 128)]
    hits = jnp.concatenate(hits, axis=1).astype(BF16)
    picked = dot16(jnp.ones((8, PICKS), BF16), hits, NT)[0:1]
    first, second = split(sketch_ref[...])
    third = sketch_ref[...] - first.astype(F32) - second.astype(F32)
    pieces = dot16(jnp.concatenate([first, second, third.astype(BF16)], axis=0), hits, NT)
    local_sketch = pieces[0:64] + (pieces[64:128] + pieces[128:192])

    sampled[...] = jnp.zeros((CAP, COLS), F32)
    for half in range(2):
        loads[3 + 2 * half].wait()
        loads[4 + 2 * half].wait()

        @pl.loop(0, 4, unroll=True)
        def _(k, half=half):
            at = pl.ds(pl.multiple_of(half * HALF + k * 256, 256), 256)
            res = values[at, :] - previous[at, :]
            high, low = split(res)
            to = (pl.ds(pl.multiple_of(k * 256, 256), 256), pl.ds(half * 128, 128))
            res_high[to] = high
            res_low[to] = low
            rest = (res - high.astype(F32) - low.astype(F32)).astype(BF16)
            line = iota((CAP, 128), 1) + (half * HALF + k * 256)
            rows = [(chosen_ref[...] == line + i * 128).astype(F32) for i in range(2)]
            rows = jnp.concatenate(rows, axis=1).astype(BF16)
            both = dot16(rows, jnp.concatenate([high, low], axis=1))
            sampled[...] += both[:, 0:128] + (both[:, 128:256] + dot16(rows, rest))

    part = dot(local_sketch, sampled[...], NT)
    for h in range(2):
        sk_part[h] = part[:, h * 128 : h * 128 + 128]
    loads[7].wait()

    pl.semaphore_wait(barrier, 32)
    copy = send(sk_part.at[1 - core], sk_core, t1_s.at[0], t1_r.at[0], sibling)
    here = pl.ds(pl.multiple_of(core * 128, 128), 128)
    there = pl.ds(pl.multiple_of((1 - core) * 128, 128), 128)
    rows_copy = send(sampled.at[there, :], sib_rows, t1_s.at[1], t1_r.at[1], sibling)
    copy.wait_recv()
    sk_mine[...] = sk_part[core] + sk_core[...]
    copies = [
        send(sk_mine, sk_in.at[d], t2_s.at[d], t2_r.at[d], (s, chip_peer(d) * 2 + core))
        for d in range(1, 8)
    ]
    total = sk_mine[...]
    for copy in copies:
        copy.wait_recv()
    for d in range(1, 8):
        total = total + sk_in[d]
    rows_copy.wait_recv()

    both = dot(total, jnp.concatenate([sampled[here, :], sib_rows[...]], axis=1))
    for i in range(2):
        rf_part[i] = both[:, i * COLS : i * COLS + COLS].reshape(8, 8, COLS)
    copies = [
        send(
            rf_part.at[1, lax.rem(member + d + swap(group), 8)], rf_in.at[1, d],
            s1_s.at[1, d], s1_r.at[1, d], (near(d), sibling[1]),
        )
        for d in range(8)
    ]
    copies += [
        send(
            rf_part.at[0, lax.rem(member + d + swap(group), 8)], rf_in.at[0, d],
            s1_s.at[0, d], s1_r.at[0, d], (near(d), t),
        )
        for d in range(1, 8)
    ]
    total = rf_part[0, chunk]
    for copy in copies:
        copy.wait_recv()
    for d in range(1, 8):
        total = total + rf_in[0, d]
    for d in range(8):
        total = total + rf_in[1, d]
    rf_group[...] = total
    copies = [
        send(rf_group, rf_far.at[d], s2_s.at[d], s2_r.at[d], (far(d), t)) for d in range(1, 4)
    ]
    settle(3)
    for copy in copies:
        copy.wait_recv()
    for d in range(1, 4):
        total = total + rf_far[d]
    rf_full[chunk] = total
    copies = [
        send(rf_full.at[chunk], rf_full.at[chunk], s3_s.at[d], s3_r.at[d], (near(d), t))
        for d in range(1, 8)
    ]
    settle(7)
    for copy in copies:
        copy.wait_recv()

    right = rf_full[...].reshape(RANK, COLS)
    masked = right * picked
    mask_high, mask_low = split(masked)
    mask_high = twice(mask_high)
    mask_both = jnp.concatenate([mask_high, twice(mask_low)], axis=0)

    def panel_piece(half, i):
        at = pl.ds(pl.multiple_of(half * 512 + i * 256, 256), 256)
        value = dot16(res_high[at, :], mask_both, NT)
        value = value[:, 0:128] + (value[:, 128:256] + dot16(res_low[at, :], mask_high, NT))
        return value.reshape(8, 32, 128)

    gram = dot(masked, right, NT)
    g_part[...] = jnp.concatenate([gram[0:32], gram[32:64]], axis=1).reshape(2, 16, 128)
    gram_copy = send(g_part.at[1 - core], g_core, gc_s.at[0], gc_r.at[0], sibling)
    panel_copies = []
    for i in range(2):
        other[i] = panel_piece(1 - core, i)
        panel_copies.append(send(other.at[i], from_core.at[i], c_s.at[i], c_r.at[i], sibling))
    gram_copy.wait_recv()
    g_half[...] = g_part[core] + g_core[...]
    gram_copies = [
        send(g_half, g_in.at[d], g_s.at[d], g_r.at[d], (s, chip_peer(d) * 2 + core))
        for d in range(1, 8)
    ]

    chip_copies = []
    for i in range(2):
        own = panel_piece(core, i)
        panel_copies[i].wait_recv()
        mine[i] = own + from_core[i]
        chip_copies.append(
            [
                send(
                    mine.at[i, chip_peer(d)], chips_in.at[i, d], p1_s.at[i, d], p1_r.at[i, d],
                    (s, chip_peer(d) * 2 + core),
                )
                for d in range(1, 8)
            ]
        )
    settle(21)
    total = g_half[...]
    for d in range(1, 8):
        gram_copies[d - 1].wait_recv()
        total = total + g_in[d]
    g_full[core] = total
    gram_copy = send(g_full.at[core], g_full.at[core], gc_s.at[1], gc_r.at[1], sibling)
    gathers = []
    for i in range(2):
        total = mine[i, chip]
        for d in range(1, 8):
            chip_copies[i][d - 1].wait_recv()
        for d in range(1, 8):
            total = total + chips_in[i, d]
        panel[core, i, chip] = total
        place = panel.at[core, i, chip]
        gathers.append(
            [
                send(place, place, p2_s.at[i, d], p2_r.at[i, d], (s, chip_peer(d) * 2 + core))
                for d in range(1, 8)
            ]
        )

    gram_copy.wait_recv()
    packed = g_full[...].reshape(32, 128)
    zero = jnp.zeros((32, 64), F32)
    top = jnp.concatenate([packed[:, 0:64], zero], axis=1)
    low = jnp.concatenate([packed[:, 64:128], zero], axis=1)
    solved = solve(
        (top[0:8], jnp.concatenate([top[8:], low], axis=0)), (right[0:8], right[8:])
    )
    high, low = split(solved)
    high, low = twice(high), twice(low)

    def low_rank_piece(half, i):
        rows = panel[half, i].reshape(256, 128)
        rows_high, rows_low = split(rows)
        value = dot16(rows_high, high) + (dot16(rows_high, low) + dot16(rows_low, high))
        at = pl.ds(pl.multiple_of(half * 512 + i * 256, 256), 256)
        for k in range(2):
            low_ref[k, at, :] = value[:, k * COLS : k * COLS + COLS]

    settle(14)
    for i in range(2):
        for copy in gathers[i]:
            copy.wait_recv()
        place = panel.at[core, i]
        handed = send(place, place, p3_s.at[i], p3_r.at[i], sibling)
        low_rank_piece(core, i)
        if i == 1:
            settle(1)
        handed.wait_recv()
        low_rank_piece(1 - core, i)
    settle()


def last_kernel(low_ref, values_ref, bounds_ref, low_rank_ref, sparse_ref):
    bound = bounds_ref[...]
    low_rank = low_ref[...]
    gap = values_ref[...] - low_rank
    low_rank_ref[...] = low_rank
    sparse_ref[...] = gap - jnp.minimum(jnp.maximum(gap, -bound), bound)


def on_device(series_values, previous_sparse, row_picks, tick_picks, sketch, thresholds):
    vmem = pl.BlockSpec(memory_space=pltpu.VMEM)
    hbm = pl.BlockSpec(memory_space=pltpu.HBM)
    dma = pltpu.SemaphoreType.DMA
    low, values, bounds = pl.pallas_call(
        main_kernel,
        out_shape=(
            jax.ShapeDtypeStruct((2, HALF, COLS), F32),
            jax.ShapeDtypeStruct((ROWS, COLS), F32),
            jax.ShapeDtypeStruct((1, COLS), F32),
        ),
        in_specs=[hbm] * 6,
        out_specs=(vmem,) * 3,
        scratch_shapes=[
            pltpu.VMEM((ROWS, COLS), F32),
            pltpu.VMEM((16, 128), jnp.int32),
            pltpu.VMEM((PICKS // 128, 128), jnp.int32),
            pltpu.VMEM((RANK, PICKS), F32),
            pltpu.VMEM((16, 128), F32),
            pltpu.VMEM((16, 128), F32),
            pltpu.VMEM((CAP, 128), jnp.int32),
            pltpu.VMEM((HALF, 2 * COLS), BF16),
            pltpu.VMEM((HALF, 2 * COLS), BF16),
            pltpu.VMEM((CAP, COLS), F32),
            pltpu.VMEM((2, RANK, 128), F32),
            pltpu.VMEM((RANK, 128), F32),
            pltpu.VMEM((RANK, 128), F32),
            pltpu.VMEM((8, RANK, 128), F32),
            pltpu.VMEM((128, COLS), F32),
            pltpu.VMEM((2, 8, 8, COLS), F32),
            pltpu.VMEM((2, 8, 8, COLS), F32),
            pltpu.VMEM((8, COLS), F32),
            pltpu.VMEM((4, 8, COLS), F32),
            pltpu.VMEM((8, 8, COLS), F32),
            pltpu.VMEM((2, 8, 32, 128), F32),
            pltpu.VMEM((2, 8, 32, 128), F32),
            pltpu.VMEM((2, 8, 32, 128), F32),
            pltpu.VMEM((2, 8, 32, 128), F32),
            pltpu.VMEM((2, 2, 8, 32, 128), F32),
            pltpu.VMEM((2, 16, 128), F32),
            pltpu.VMEM((16, 128), F32),
            pltpu.VMEM((16, 128), F32),
            pltpu.VMEM((8, 16, 128), F32),
            pltpu.VMEM((2, 16, 128), F32),
            dma((8,)),
            dma((2,)), dma((2,)), dma((8,)), dma((8,)),
            dma((2, 8)), dma((2, 8)), dma((4,)), dma((4,)), dma((8,)), dma((8,)),
            dma((2,)), dma((2,)), dma((2, 8)), dma((2, 8)), dma((2, 8)), dma((2, 8)),
            dma((2,)), dma((2,)),
            dma((8,)), dma((8,)), dma((2,)), dma((2,)),
        ],
        compiler_params=pltpu.CompilerParams(
            collective_id=0, has_side_effects=True, vmem_limit_bytes=24 << 20
        ),
        name="cur_core",
    )(
        *(
            pltpu.with_memory_space_constraint(x, pltpu.HBM)
            for x in (
                series_values,
                previous_sparse,
                row_picks.reshape(16, 128),
                tick_picks.reshape(PICKS // 128, 128),
                sketch.T,
                thresholds.reshape(1, COLS),
            )
        )
    )
    steps = 2
    block = pl.BlockSpec((ROWS // steps, COLS), lambda i: (i, 0))
    return pl.pallas_call(
        last_kernel,
        grid=(steps,),
        out_shape=(jax.ShapeDtypeStruct((ROWS, COLS), F32),) * 2,
        in_specs=[block, block, pl.BlockSpec((1, COLS), lambda i: (0, 0))],
        out_specs=(block, block),
        compiler_params=pltpu.CompilerParams(vmem_limit_bytes=16 << 20),
        name="low_rank_and_sparse",
    )(low.reshape(ROWS, COLS), values, bounds)


def solution(mesh):
    placed = (P("series", "tick"), P("series", "tick"), P(), P(), P(), P("tick"))
    return jax.shard_map(
        on_device,
        mesh=mesh,
        in_specs=placed,
        out_specs=(P("series", "tick"), P("series", "tick")),
        check_vma=False,
    )
```

```python
import jax
import jax.numpy as jnp
from jax import lax
from jax.experimental import pallas as pl
from jax.experimental.pallas import tpu as pltpu
from jax.sharding import PartitionSpec as P

CAP = 256
RANK = 64
ROWS = 2048
COLS = 128
PICKS = 512
HALF = ROWS // 2
NN = (((1,), (0,)), ((), ()))
NT = (((1,), (1,)), ((), ()))
F32 = jnp.float32
BF16 = jnp.bfloat16


def dot(a, b, dims=NN):
    return lax.dot_general(
        a, b, dims, precision=lax.Precision.HIGHEST, preferred_element_type=F32
    )


def dot16(a, b, dims=NN):
    return lax.dot_general(
        a, b, dims, precision=lax.Precision.DEFAULT, preferred_element_type=F32
    )


def iota(shape, dim):
    return lax.broadcasted_iota(jnp.int32, shape, dim)


def split(x):
    high = x.astype(BF16)
    return high, (x - high.astype(F32)).astype(BF16)


def twice(x):
    zero = jnp.zeros_like(x)
    return jnp.concatenate(
        [jnp.concatenate([x, zero], axis=1), jnp.concatenate([zero, x], axis=1)], axis=0
    )


def find_rows(picks, row_start, slot_ref, mark_ref):
    local = picks - row_start
    inside = (local >= 0) & (local < ROWS)
    flags = jnp.where(inside, 1.0, 0.0).astype(BF16)
    upto = (iota((128, 128), 0) <= iota((128, 128), 1)).astype(F32).astype(BF16)
    along = dot16(flags, upto)
    total = dot16(flags, jnp.ones((128, 128), BF16))
    before = (iota((16, 16), 1) < iota((16, 16), 0)).astype(F32).astype(BF16)
    ahead = dot16(before, total.astype(BF16))
    slot_ref[...] = jnp.where(inside, along + ahead - 1.0, -1.0)
    mark_ref[...] = jnp.where(inside, local + 1, 0).astype(F32)
    lines = iota((CAP, 128), 0).astype(F32)

    def one(i, found):
        return found + jnp.where(slot_ref[pl.ds(i, 1), :] == lines, mark_ref[pl.ds(i, 1), :], 0.0)

    found = lax.fori_loop(0, 16, one, jnp.zeros((CAP, 128), F32))
    return (jnp.sum(found, axis=1, keepdims=True) - 1.0).astype(jnp.int32)


def solve(a, x):
    lines = iota((8, 128), 0)

    def round_of_8(_, state):
        a, x = state
        columns = [
            tuple(jnp.broadcast_to(part[:, k : k + 1], (part.shape[0], 128)) for part in a)
            for k in range(8)
        ]
        for k in range(8):
            top, rest = columns[k]
            inverse = 1.0 / top[k : k + 1, :]

            def eliminate(both, top=top, rest=rest, inverse=inverse, k=k):
                row = both[0][k : k + 1, :] * inverse
                return jnp.where(lines == k, row, both[0] - top * row), both[1] - rest * row

            columns = [c if i <= k else eliminate(c) for i, c in enumerate(columns)]
            a, x = eliminate(a), eliminate(x)
        a, x = (
            (both[1][0:8], jnp.concatenate([both[1][8:], both[0]], axis=0)) for both in (a, x)
        )
        return tuple(pltpu.roll(part, 120, 1) for part in a), x

    return jnp.concatenate(lax.fori_loop(0, RANK // 8, round_of_8, (a, x))[1], axis=0)


def main_kernel(
    series_hbm, sparse_hbm, row_hbm, tick_hbm, sketch_hbm, bound_hbm,
    low_ref, values, bounds,
    previous, row_ref, tick_ref, sketch_ref, slot_ref, mark_ref, chosen_ref,
    res_high, res_low, sampled, sk_part, sk_core, sk_mine, sk_in, sib_rows,
    rf_part, rf_in, rf_group, rf_far, rf_full,
    other, mine, from_core, chips_in, panel, g_part, g_core, g_half, g_in, g_full,
    in_sem, t1_s, t1_r, t2_s, t2_r, s1_s, s1_r, s2_s, s2_r, s3_s, s3_r,
    c_s, c_r, p1_s, p1_r, p2_s, p2_r, p3_s, p3_r, g_s, g_r, gc_s, gc_r,
):
    s = lax.axis_index("series")
    t = lax.axis_index("tick")
    member, group = lax.rem(s, 8), s // 8
    chip, core = t // 2, lax.rem(t, 2)
    sibling = (s, t + 1 - 2 * core)

    def swap(g):
        return 2 * (g // 2)

    base = lax.rem(member + 6, 8)
    edge = base // 4
    chunk = lax.rem(base + swap(group), 4)

    def near(d):
        return group * 8 + lax.rem(member + d, 8)

    def owner(j):
        return group * 8 + 2 + lax.rem(j + swap(group), 4)

    def far(d):
        g = lax.rem(group + d, 4)
        return g * 8 + edge * member + (1 - edge) * (2 + lax.rem(chunk + swap(g), 4))

    def chip_peer(d):
        return lax.rem(chip + d, 8)

    def send(src, dst, send_sem, recv_sem, device):
        copy = pltpu.make_async_remote_copy(
            src_ref=src, dst_ref=dst, send_sem=send_sem, recv_sem=recv_sem,
            device_id=device, device_id_type=pl.DeviceIdType.MESH,
        )
        copy.start()
        sent.append(copy)
        return copy

    sent = []

    def settle(keep=0):
        while len(sent) > keep:
            sent.pop(0).wait_send()

    barrier = pltpu.get_barrier_semaphore()

    def greet(device):
        pl.semaphore_signal(barrier, inc=1, device_id=device, device_id_type=pl.DeviceIdType.MESH)

    loads = []
    for i, (src, dst) in enumerate(
        [
            (row_hbm, row_ref), (tick_hbm, tick_ref), (sketch_hbm, sketch_ref),
            (series_hbm.at[0:HALF], values.at[0:HALF]),
            (sparse_hbm.at[0:HALF], previous.at[0:HALF]),
            (series_hbm.at[HALF:ROWS], values.at[HALF:ROWS]),
            (sparse_hbm.at[HALF:ROWS], previous.at[HALF:ROWS]),
            (bound_hbm, bounds),
        ]
    ):
        load = pltpu.make_async_copy(src, dst, in_sem.at[i])
        load.start()
        loads.append(load)

    for d in range(1, 16):
        greet((s, lax.rem(t + d, 16)))
    for d in range(1, 8):
        greet((near(d), t))
        greet((near(d), sibling[1]))
    for d in range(1, 4):
        greet((far(d), t))

    loads[0].wait()
    chosen = find_rows(row_ref[...], s * ROWS, slot_ref, mark_ref)
    chosen_ref[...] = jnp.broadcast_to(chosen, (CAP, 128))
    loads[1].wait()
    loads[2].wait()
    ticks = iota((COLS, 128), 0) + t * COLS
    hits = [(ticks == tick_ref[i : i + 1, :]).astype(F32) for i in range(PICKS // 128)]
    hits = jnp.concatenate(hits, axis=1).astype(BF16)
    picked = dot16(jnp.ones((8, PICKS), BF16), hits, NT)[0:1]
    first, second = split(sketch_ref[...])
    third = sketch_ref[...] - first.astype(F32) - second.astype(F32)
    pieces = dot16(jnp.concatenate([first, second, third.astype(BF16)], axis=0), hits, NT)
    local_sketch = pieces[0:64] + (pieces[64:128] + pieces[128:192])

    sampled[...] = jnp.zeros((CAP, COLS), F32)
    for half in range(2):
        loads[3 + 2 * half].wait()
        loads[4 + 2 * half].wait()

        @pl.loop(0, 4, unroll=True)
        def _(k, half=half):
            at = pl.ds(pl.multiple_of(half * HALF + k * 256, 256), 256)
            res = values[at, :] - previous[at, :]
            high, low = split(res)
            to = (pl.ds(pl.multiple_of(k * 256, 256), 256), pl.ds(half * 128, 128))
            res_high[to] = high
            res_low[to] = low
            rest = (res - high.astype(F32) - low.astype(F32)).astype(BF16)
            line = iota((CAP, 128), 1) + (half * HALF + k * 256)
            rows = [(chosen_ref[...] == line + i * 128).astype(F32) for i in range(2)]
            rows = jnp.concatenate(rows, axis=1).astype(BF16)
            both = dot16(rows, jnp.concatenate([high, low], axis=1))
            sampled[...] += both[:, 0:128] + (both[:, 128:256] + dot16(rows, rest))

    part = dot(local_sketch, sampled[...], NT)
    for h in range(2):
        sk_part[h] = part[:, h * 128 : h * 128 + 128]
    loads[7].wait()

    pl.semaphore_wait(barrier, 32)
    copy = send(sk_part.at[1 - core], sk_core, t1_s.at[0], t1_r.at[0], sibling)
    here = pl.ds(pl.multiple_of(core * 128, 128), 128)
    there = pl.ds(pl.multiple_of((1 - core) * 128, 128), 128)
    rows_copy = send(sampled.at[there, :], sib_rows, t1_s.at[1], t1_r.at[1], sibling)
    copy.wait_recv()
    sk_mine[...] = sk_part[core] + sk_core[...]
    copies = [
        send(sk_mine, sk_in.at[d], t2_s.at[d], t2_r.at[d], (s, chip_peer(d) * 2 + core))
        for d in range(1, 8)
    ]
    total = sk_mine[...]
    for copy in copies:
        copy.wait_recv()
    for d in range(1, 8):
        total = total + sk_in[d]
    rows_copy.wait_recv()

    both = dot(total, jnp.concatenate([sampled[here, :], sib_rows[...]], axis=1))
    for i in range(2):
        rf_part[i] = both[:, i * COLS : i * COLS + COLS].reshape(4, 16, COLS)

    def to_owner(i, q, to_tick):
        j = lax.rem(chunk + q, 4)
        return pltpu.make_async_remote_copy(
            src_ref=rf_part.at[i, j], dst_ref=rf_in.at[i, member], send_sem=s1_s.at[i, q],
            recv_sem=s1_r.at[i, member], device_id=(owner(j), to_tick),
            device_id_type=pl.DeviceIdType.MESH,
        )

    for q in range(4):
        sent.append(to_owner(1, q, sibling[1]))
        sent[-1].start()
    for q in range(1, 4):
        sent.append(to_owner(0, q, t))
        sent[-1].start()

    @pl.when(edge == 1)
    def _():
        to_owner(0, 0, t).start()

    def from_owner(j, d):
        return pltpu.make_async_remote_copy(
            src_ref=rf_full.at[j], dst_ref=rf_full.at[j], send_sem=s3_s.at[d],
            recv_sem=s3_r.at[j], device_id=(near(d), t), device_id_type=pl.DeviceIdType.MESH,
        )

    def to_far(d):
        return pltpu.make_async_remote_copy(
            src_ref=rf_group, dst_ref=rf_far.at[d], send_sem=s2_s.at[d], recv_sem=s2_r.at[d],
            device_id=(far(d), t), device_id_type=pl.DeviceIdType.MESH,
        )

    @pl.when(edge == 0)
    def _():
        total = rf_part[0, chunk]
        for i in range(2):
            for d in range(1 - i, 8):
                m = lax.rem(member + d, 8)
                pltpu.make_async_remote_copy(
                    src_ref=rf_part.at[i, 0], dst_ref=rf_in.at[i, m], send_sem=s1_s.at[i, 0],
                    recv_sem=s1_r.at[i, m], device_id=sibling,
                    device_id_type=pl.DeviceIdType.MESH,
                ).wait_recv()
                total = total + rf_in[i, m]
        rf_group[...] = total
        for d in range(1, 4):
            to_far(d).start()
        for d in range(1, 4):
            to_far(d).wait_recv()
            total = total + rf_far[d]
        rf_full[chunk] = total
        for d in range(1, 8):
            from_owner(chunk, d).start()

    settle()

    @pl.when(edge == 1)
    def _():
        to_owner(0, 0, t).wait_send()
        from_owner(chunk, 1).wait_recv()

    for q in range(1, 4):
        from_owner(lax.rem(chunk + q, 4), 1).wait_recv()

    right = rf_full[...].reshape(RANK, COLS)
    masked = right * picked
    mask_high, mask_low = split(masked)
    mask_high = twice(mask_high)
    mask_both = jnp.concatenate([mask_high, twice(mask_low)], axis=0)

    def panel_piece(half, i):
        at = pl.ds(pl.multiple_of(half * 512 + i * 256, 256), 256)
        value = dot16(res_high[at, :], mask_both, NT)
        value = value[:, 0:128] + (value[:, 128:256] + dot16(res_low[at, :], mask_high, NT))
        return value.reshape(8, 32, 128)

    gram = dot(masked, right, NT)
    g_part[...] = jnp.concatenate([gram[0:32], gram[32:64]], axis=1).reshape(2, 16, 128)
    gram_copy = send(g_part.at[1 - core], g_core, gc_s.at[0], gc_r.at[0], sibling)
    panel_copies = []
    for i in range(2):
        other[i] = panel_piece(1 - core, i)
        panel_copies.append(send(other.at[i], from_core.at[i], c_s.at[i], c_r.at[i], sibling))
    gram_copy.wait_recv()
    g_half[...] = g_part[core] + g_core[...]
    gram_copies = [
        send(g_half, g_in.at[d], g_s.at[d], g_r.at[d], (s, chip_peer(d) * 2 + core))
        for d in range(1, 8)
    ]

    chip_copies = []
    for i in range(2):
        own = panel_piece(core, i)
        panel_copies[i].wait_recv()
        mine[i] = own + from_core[i]
        chip_copies.append(
            [
                send(
                    mine.at[i, chip_peer(d)], chips_in.at[i, d], p1_s.at[i, d], p1_r.at[i, d],
                    (s, chip_peer(d) * 2 + core),
                )
                for d in range(1, 8)
            ]
        )
    settle(21)

    @pl.when(edge == 0)
    def _():
        for d in range(1, 4):
            to_far(d).wait_send()
        for d in range(1, 8):
            from_owner(chunk, d).wait_send()

    total = g_half[...]
    for d in range(1, 8):
        gram_copies[d - 1].wait_recv()
        total = total + g_in[d]
    g_full[core] = total
    gram_copy = send(g_full.at[core], g_full.at[core], gc_s.at[1], gc_r.at[1], sibling)
    gathers = []
    for i in range(2):
        total = mine[i, chip]
        for d in range(1, 8):
            chip_copies[i][d - 1].wait_recv()
        for d in range(1, 8):
            total = total + chips_in[i, d]
        panel[core, i, chip] = total
        place = panel.at[core, i, chip]
        gathers.append(
            [
                send(place, place, p2_s.at[i, d], p2_r.at[i, d], (s, chip_peer(d) * 2 + core))
                for d in range(1, 8)
            ]
        )

    gram_copy.wait_recv()
    packed = g_full[...].reshape(32, 128)
    zero = jnp.zeros((32, 64), F32)
    top = jnp.concatenate([packed[:, 0:64], zero], axis=1)
    low = jnp.concatenate([packed[:, 64:128], zero], axis=1)
    solved = solve(
        (top[0:8], jnp.concatenate([top[8:], low], axis=0)), (right[0:8], right[8:])
    )
    high, low = split(solved)
    high, low = twice(high), twice(low)

    def low_rank_piece(half, i):
        rows = panel[half, i].reshape(256, 128)
        rows_high, rows_low = split(rows)
        value = dot16(rows_high, high) + (dot16(rows_high, low) + dot16(rows_low, high))
        at = pl.ds(pl.multiple_of(half * 512 + i * 256, 256), 256)
        for k in range(2):
            low_ref[k, at, :] = value[:, k * COLS : k * COLS + COLS]

    settle(14)
    for i in range(2):
        for copy in gathers[i]:
            copy.wait_recv()
        place = panel.at[core, i]
        handed = send(place, place, p3_s.at[i], p3_r.at[i], sibling)
        low_rank_piece(core, i)
        if i == 1:
            settle(1)
        handed.wait_recv()
        low_rank_piece(1 - core, i)
    settle()


def last_kernel(low_ref, values_ref, bounds_ref, low_rank_ref, sparse_ref):
    bound = bounds_ref[...]
    low_rank = low_ref[...]
    gap = values_ref[...] - low_rank
    low_rank_ref[...] = low_rank
    sparse_ref[...] = gap - jnp.minimum(jnp.maximum(gap, -bound), bound)


def on_device(series_values, previous_sparse, row_picks, tick_picks, sketch, thresholds):
    vmem = pl.BlockSpec(memory_space=pltpu.VMEM)
    hbm = pl.BlockSpec(memory_space=pltpu.HBM)
    dma = pltpu.SemaphoreType.DMA
    low, values, bounds = pl.pallas_call(
        main_kernel,
        out_shape=(
            jax.ShapeDtypeStruct((2, HALF, COLS), F32),
            jax.ShapeDtypeStruct((ROWS, COLS), F32),
            jax.ShapeDtypeStruct((1, COLS), F32),
        ),
        in_specs=[hbm] * 6,
        out_specs=(vmem,) * 3,
        scratch_shapes=[
            pltpu.VMEM((ROWS, COLS), F32),
            pltpu.VMEM((16, 128), jnp.int32),
            pltpu.VMEM((PICKS // 128, 128), jnp.int32),
            pltpu.VMEM((RANK, PICKS), F32),
            pltpu.VMEM((16, 128), F32),
            pltpu.VMEM((16, 128), F32),
            pltpu.VMEM((CAP, 128), jnp.int32),
            pltpu.VMEM((HALF, 2 * COLS), BF16),
            pltpu.VMEM((HALF, 2 * COLS), BF16),
            pltpu.VMEM((CAP, COLS), F32),
            pltpu.VMEM((2, RANK, 128), F32),
            pltpu.VMEM((RANK, 128), F32),
            pltpu.VMEM((RANK, 128), F32),
            pltpu.VMEM((8, RANK, 128), F32),
            pltpu.VMEM((128, COLS), F32),
            pltpu.VMEM((2, 4, 16, COLS), F32),
            pltpu.VMEM((2, 8, 16, COLS), F32),
            pltpu.VMEM((16, COLS), F32),
            pltpu.VMEM((4, 16, COLS), F32),
            pltpu.VMEM((4, 16, COLS), F32),
            pltpu.VMEM((2, 8, 32, 128), F32),
            pltpu.VMEM((2, 8, 32, 128), F32),
            pltpu.VMEM((2, 8, 32, 128), F32),
            pltpu.VMEM((2, 8, 32, 128), F32),
            pltpu.VMEM((2, 2, 8, 32, 128), F32),
            pltpu.VMEM((2, 16, 128), F32),
            pltpu.VMEM((16, 128), F32),
            pltpu.VMEM((16, 128), F32),
            pltpu.VMEM((8, 16, 128), F32),
            pltpu.VMEM((2, 16, 128), F32),
            dma((8,)),
            dma((2,)), dma((2,)), dma((8,)), dma((8,)),
            dma((2, 4)), dma((2, 8)), dma((4,)), dma((4,)), dma((8,)), dma((4,)),
            dma((2,)), dma((2,)), dma((2, 8)), dma((2, 8)), dma((2, 8)), dma((2, 8)),
            dma((2,)), dma((2,)),
            dma((8,)), dma((8,)), dma((2,)), dma((2,)),
        ],
        compiler_params=pltpu.CompilerParams(
            collective_id=0, has_side_effects=True, vmem_limit_bytes=24 << 20
        ),
        name="cur_core",
    )(
        *(
            pltpu.with_memory_space_constraint(x, pltpu.HBM)
            for x in (
                series_values,
                previous_sparse,
                row_picks.reshape(16, 128),
                tick_picks.reshape(PICKS // 128, 128),
                sketch.T,
                thresholds.reshape(1, COLS),
            )
        )
    )
    steps = 2
    block = pl.BlockSpec((ROWS // steps, COLS), lambda i: (i, 0))
    return pl.pallas_call(
        last_kernel,
        grid=(steps,),
        out_shape=(jax.ShapeDtypeStruct((ROWS, COLS), F32),) * 2,
        in_specs=[block, block, pl.BlockSpec((1, COLS), lambda i: (0, 0))],
        out_specs=(block, block),
        compiler_params=pltpu.CompilerParams(vmem_limit_bytes=16 << 20),
        name="low_rank_and_sparse",
    )(low.reshape(ROWS, COLS), values, bounds)


def solution(mesh):
    placed = (P("series", "tick"), P("series", "tick"), P(), P(), P(), P("tick"))
    return jax.shard_map(
        on_device,
        mesh=mesh,
        in_specs=placed,
        out_specs=(P("series", "tick"), P("series", "tick")),
        check_vma=False,
    )
```

```python
import jax
import jax.numpy as jnp
from jax import lax
from jax.experimental import pallas as pl
from jax.experimental.pallas import tpu as pltpu
from jax.sharding import PartitionSpec as P

CAP = 256
RANK = 64
ROWS = 2048
COLS = 128
PICKS = 512
HALF = ROWS // 2
NN = (((1,), (0,)), ((), ()))
NT = (((1,), (1,)), ((), ()))
F32 = jnp.float32
BF16 = jnp.bfloat16


def dot(a, b, dims=NN):
    return lax.dot_general(
        a, b, dims, precision=lax.Precision.HIGHEST, preferred_element_type=F32
    )


def dot16(a, b, dims=NN):
    return lax.dot_general(
        a, b, dims, precision=lax.Precision.DEFAULT, preferred_element_type=F32
    )


def dot_parts(a, b, dims=NN):
    (a_high, a_low), (b_high, b_low) = split(a), split(b)
    return dot16(a_high, b_high, dims) + (dot16(a_high, b_low, dims) + dot16(a_low, b_high, dims))


def iota(shape, dim):
    return lax.broadcasted_iota(jnp.int32, shape, dim)


def split(x):
    high = x.astype(BF16)
    return high, (x - high.astype(F32)).astype(BF16)


def twice(x):
    zero = jnp.zeros_like(x)
    return jnp.concatenate(
        [jnp.concatenate([x, zero], axis=1), jnp.concatenate([zero, x], axis=1)], axis=0
    )


def find_rows(picks, row_start, slot_ref, mark_ref):
    local = picks - row_start
    inside = (local >= 0) & (local < ROWS)
    flags = jnp.where(inside, 1.0, 0.0).astype(BF16)
    upto = (iota((128, 128), 0) <= iota((128, 128), 1)).astype(F32).astype(BF16)
    along = dot16(flags, upto)
    total = dot16(flags, jnp.ones((128, 128), BF16))
    before = (iota((16, 16), 1) < iota((16, 16), 0)).astype(F32).astype(BF16)
    ahead = dot16(before, total.astype(BF16))
    slot_ref[...] = jnp.where(inside, along + ahead - 1.0, -1.0)
    mark_ref[...] = jnp.where(inside, local + 1, 0).astype(F32)
    lines = iota((CAP, 128), 0).astype(F32)

    def one(i, found):
        return found + jnp.where(slot_ref[pl.ds(i, 1), :] == lines, mark_ref[pl.ds(i, 1), :], 0.0)

    found = lax.fori_loop(0, 16, one, jnp.zeros((CAP, 128), F32))
    return (jnp.sum(found, axis=1, keepdims=True) - 1.0).astype(jnp.int32)


def solve(a, x):
    lines = iota((8, 128), 0)

    def round_of_8(_, state):
        a, x = state
        columns = [
            tuple(jnp.broadcast_to(part[:, k : k + 1], (part.shape[0], 128)) for part in a)
            for k in range(8)
        ]
        for k in range(8):
            top, rest = columns[k]
            inverse = 1.0 / top[k : k + 1, :]

            def eliminate(both, top=top, rest=rest, inverse=inverse, k=k):
                row = both[0][k : k + 1, :] * inverse
                return jnp.where(lines == k, row, both[0] - top * row), both[1] - rest * row

            columns = [c if i <= k else eliminate(c) for i, c in enumerate(columns)]
            a, x = eliminate(a), eliminate(x)
        a, x = (
            (both[1][0:8], jnp.concatenate([both[1][8:], both[0]], axis=0)) for both in (a, x)
        )
        return tuple(pltpu.roll(part, 120, 1) for part in a), x

    return jnp.concatenate(lax.fori_loop(0, RANK // 8, round_of_8, (a, x))[1], axis=0)


def main_kernel(
    series_hbm, sparse_hbm, row_hbm, tick_hbm, sketch_hbm, bound_hbm,
    low_ref, values, bounds,
    previous, row_ref, tick_ref, sketch_ref, slot_ref, mark_ref, chosen_ref,
    res_high, res_low, sampled, sk_part, sk_core, sk_mine, sk_in, sib_rows,
    rf_part, rf_in, rf_group, rf_far, rf_full,
    other, mine, from_core, chips_in, panel, g_part, g_core, g_half, g_in, g_full,
    in_sem, t1_s, t1_r, t2_s, t2_r, s1_s, s1_r, s2_s, s2_r, s3_s, s3_r,
    c_s, c_r, p1_s, p1_r, p2_s, p2_r, p3_s, p3_r, g_s, g_r, gc_s, gc_r,
):
    s = lax.axis_index("series")
    t = lax.axis_index("tick")
    member, group = lax.rem(s, 8), s // 8
    chip, core = t // 2, lax.rem(t, 2)
    sibling = (s, t + 1 - 2 * core)

    def swap(g):
        return 2 * (g // 2)

    base = lax.rem(member + 6, 8)
    edge = base // 4
    chunk = lax.rem(base + swap(group), 4)

    def near(d):
        return group * 8 + lax.rem(member + d, 8)

    def owner(j):
        return group * 8 + 2 + lax.rem(j + swap(group), 4)

    def far(d):
        g = lax.rem(group + d, 4)
        return g * 8 + edge * member + (1 - edge) * (2 + lax.rem(chunk + swap(g), 4))

    def chip_peer(d):
        return lax.rem(chip + d, 8)

    def send(src, dst, send_sem, recv_sem, device):
        copy = pltpu.make_async_remote_copy(
            src_ref=src, dst_ref=dst, send_sem=send_sem, recv_sem=recv_sem,
            device_id=device, device_id_type=pl.DeviceIdType.MESH,
        )
        copy.start()
        sent.append(copy)
        return copy

    sent = []

    def settle(keep=0):
        while len(sent) > keep:
            sent.pop(0).wait_send()

    barrier = pltpu.get_barrier_semaphore()

    def greet(device):
        pl.semaphore_signal(barrier, inc=1, device_id=device, device_id_type=pl.DeviceIdType.MESH)

    loads = []
    for i, (src, dst) in enumerate(
        [
            (row_hbm, row_ref), (tick_hbm, tick_ref), (sketch_hbm, sketch_ref),
            (series_hbm.at[0:HALF], values.at[0:HALF]),
            (sparse_hbm.at[0:HALF], previous.at[0:HALF]),
            (series_hbm.at[HALF:ROWS], values.at[HALF:ROWS]),
            (sparse_hbm.at[HALF:ROWS], previous.at[HALF:ROWS]),
            (bound_hbm, bounds),
        ]
    ):
        load = pltpu.make_async_copy(src, dst, in_sem.at[i])
        load.start()
        loads.append(load)

    for d in range(1, 16):
        greet((s, lax.rem(t + d, 16)))
    for d in range(1, 8):
        greet((near(d), t))
        greet((near(d), sibling[1]))
    for d in range(1, 4):
        greet((far(d), t))

    loads[0].wait()
    chosen = find_rows(row_ref[...], s * ROWS, slot_ref, mark_ref)
    chosen_ref[...] = jnp.broadcast_to(chosen, (CAP, 128))
    loads[1].wait()
    loads[2].wait()
    ticks = iota((COLS, 128), 0) + t * COLS
    hits = [(ticks == tick_ref[i : i + 1, :]).astype(F32) for i in range(PICKS // 128)]
    hits = jnp.concatenate(hits, axis=1).astype(BF16)
    picked = dot16(jnp.ones((8, PICKS), BF16), hits, NT)[0:1]
    first, second = split(sketch_ref[...])
    third = sketch_ref[...] - first.astype(F32) - second.astype(F32)
    pieces = dot16(jnp.concatenate([first, second, third.astype(BF16)], axis=0), hits, NT)
    local_sketch = pieces[0:64] + (pieces[64:128] + pieces[128:192])

    sampled[...] = jnp.zeros((CAP, COLS), F32)
    for half in range(2):
        loads[3 + 2 * half].wait()
        loads[4 + 2 * half].wait()

        @pl.loop(0, 4, unroll=True)
        def _(k, half=half):
            at = pl.ds(pl.multiple_of(half * HALF + k * 256, 256), 256)
            res = values[at, :] - previous[at, :]
            high, low = split(res)
            to = (pl.ds(pl.multiple_of(k * 256, 256), 256), pl.ds(half * 128, 128))
            res_high[to] = high
            res_low[to] = low
            rest = (res - high.astype(F32) - low.astype(F32)).astype(BF16)
            line = iota((CAP, 128), 1) + (half * HALF + k * 256)
            rows = [(chosen_ref[...] == line + i * 128).astype(F32) for i in range(2)]
            rows = jnp.concatenate(rows, axis=1).astype(BF16)
            both = dot16(rows, jnp.concatenate([high, low], axis=1))
            sampled[...] += both[:, 0:128] + (both[:, 128:256] + dot16(rows, rest))

    part = dot_parts(local_sketch, sampled[...], NT)
    for h in range(2):
        sk_part[h] = part[:, h * 128 : h * 128 + 128]
    loads[7].wait()

    pl.semaphore_wait(barrier, 32)
    copy = send(sk_part.at[1 - core], sk_core, t1_s.at[0], t1_r.at[0], sibling)
    here = pl.ds(pl.multiple_of(core * 128, 128), 128)
    there = pl.ds(pl.multiple_of((1 - core) * 128, 128), 128)
    rows_copy = send(sampled.at[there, :], sib_rows, t1_s.at[1], t1_r.at[1], sibling)
    copy.wait_recv()
    sk_mine[...] = sk_part[core] + sk_core[...]
    copies = [
        send(sk_mine, sk_in.at[d], t2_s.at[d], t2_r.at[d], (s, chip_peer(d) * 2 + core))
        for d in range(1, 8)
    ]
    total = sk_mine[...]
    for copy in copies:
        copy.wait_recv()
    for d in range(1, 8):
        total = total + sk_in[d]
    rows_copy.wait_recv()

    both = dot_parts(total, jnp.concatenate([sampled[here, :], sib_rows[...]], axis=1))
    for i in range(2):
        rf_part[i] = both[:, i * COLS : i * COLS + COLS].reshape(4, 16, COLS)

    def to_owner(i, q, to_tick):
        j = lax.rem(chunk + q, 4)
        return pltpu.make_async_remote_copy(
            src_ref=rf_part.at[i, j], dst_ref=rf_in.at[i, member], send_sem=s1_s.at[i, q],
            recv_sem=s1_r.at[i, member], device_id=(owner(j), to_tick),
            device_id_type=pl.DeviceIdType.MESH,
        )

    for q in range(4):
        sent.append(to_owner(1, q, sibling[1]))
        sent[-1].start()
    for q in range(1, 4):
        sent.append(to_owner(0, q, t))
        sent[-1].start()

    @pl.when(edge == 1)
    def _():
        to_owner(0, 0, t).start()

    def from_owner(j, d):
        return pltpu.make_async_remote_copy(
            src_ref=rf_full.at[j], dst_ref=rf_full.at[j], send_sem=s3_s.at[d],
            recv_sem=s3_r.at[j], device_id=(near(d), t), device_id_type=pl.DeviceIdType.MESH,
        )

    def to_far(d):
        return pltpu.make_async_remote_copy(
            src_ref=rf_group, dst_ref=rf_far.at[d], send_sem=s2_s.at[d], recv_sem=s2_r.at[d],
            device_id=(far(d), t), device_id_type=pl.DeviceIdType.MESH,
        )

    @pl.when(edge == 0)
    def _():
        total = rf_part[0, chunk]
        for i in range(2):
            for d in range(1 - i, 8):
                m = lax.rem(member + d, 8)
                pltpu.make_async_remote_copy(
                    src_ref=rf_part.at[i, 0], dst_ref=rf_in.at[i, m], send_sem=s1_s.at[i, 0],
                    recv_sem=s1_r.at[i, m], device_id=sibling,
                    device_id_type=pl.DeviceIdType.MESH,
                ).wait_recv()
                total = total + rf_in[i, m]
        rf_group[...] = total
        for d in range(1, 4):
            to_far(d).start()
        for d in range(1, 4):
            to_far(d).wait_recv()
            total = total + rf_far[d]
        rf_full[chunk] = total
        for d in range(1, 8):
            from_owner(chunk, d).start()

    settle()

    @pl.when(edge == 1)
    def _():
        to_owner(0, 0, t).wait_send()
        from_owner(chunk, 1).wait_recv()

    for q in range(1, 4):
        from_owner(lax.rem(chunk + q, 4), 1).wait_recv()

    right = rf_full[...].reshape(RANK, COLS)
    masked = right * picked
    mask_high, mask_low = split(masked)
    mask_high = twice(mask_high)
    mask_both = jnp.concatenate([mask_high, twice(mask_low)], axis=0)

    def panel_piece(half, i):
        at = pl.ds(pl.multiple_of(half * 512 + i * 256, 256), 256)
        value = dot16(res_high[at, :], mask_both, NT)
        value = value[:, 0:128] + (value[:, 128:256] + dot16(res_low[at, :], mask_high, NT))
        return value.reshape(8, 32, 128)

    gram = dot(masked, right, NT)
    g_part[...] = jnp.concatenate([gram[0:32], gram[32:64]], axis=1).reshape(2, 16, 128)
    gram_copy = send(g_part.at[1 - core], g_core, gc_s.at[0], gc_r.at[0], sibling)
    panel_copies = []
    for i in range(2):
        other[i] = panel_piece(1 - core, i)
        panel_copies.append(send(other.at[i], from_core.at[i], c_s.at[i], c_r.at[i], sibling))
    gram_copy.wait_recv()
    g_half[...] = g_part[core] + g_core[...]
    gram_copies = [
        send(g_half, g_in.at[d], g_s.at[d], g_r.at[d], (s, chip_peer(d) * 2 + core))
        for d in range(1, 8)
    ]

    chip_copies = []
    for i in range(2):
        own = panel_piece(core, i)
        panel_copies[i].wait_recv()
        mine[i] = own + from_core[i]
        chip_copies.append(
            [
                send(
                    mine.at[i, chip_peer(d)], chips_in.at[i, d], p1_s.at[i, d], p1_r.at[i, d],
                    (s, chip_peer(d) * 2 + core),
                )
                for d in range(1, 8)
            ]
        )
    settle(21)

    @pl.when(edge == 0)
    def _():
        for d in range(1, 4):
            to_far(d).wait_send()
        for d in range(1, 8):
            from_owner(chunk, d).wait_send()

    total = g_half[...]
    for d in range(1, 8):
        gram_copies[d - 1].wait_recv()
        total = total + g_in[d]
    g_full[core] = total
    gram_copy = send(g_full.at[core], g_full.at[core], gc_s.at[1], gc_r.at[1], sibling)
    gathers = []
    for i in range(2):
        total = mine[i, chip]
        for d in range(1, 8):
            chip_copies[i][d - 1].wait_recv()
        for d in range(1, 8):
            total = total + chips_in[i, d]
        panel[core, i, chip] = total
        place = panel.at[core, i, chip]
        gathers.append(
            [
                send(place, place, p2_s.at[i, d], p2_r.at[i, d], (s, chip_peer(d) * 2 + core))
                for d in range(1, 8)
            ]
        )

    gram_copy.wait_recv()
    packed = g_full[...].reshape(32, 128)
    zero = jnp.zeros((32, 64), F32)
    top = jnp.concatenate([packed[:, 0:64], zero], axis=1)
    low = jnp.concatenate([packed[:, 64:128], zero], axis=1)
    solved = solve(
        (top[0:8], jnp.concatenate([top[8:], low], axis=0)), (right[0:8], right[8:])
    )
    high, low = split(solved)
    high, low = twice(high), twice(low)

    def low_rank_piece(half, i):
        rows = panel[half, i].reshape(256, 128)
        rows_high, rows_low = split(rows)
        value = dot16(rows_high, high) + (dot16(rows_high, low) + dot16(rows_low, high))
        at = pl.ds(pl.multiple_of(half * 512 + i * 256, 256), 256)
        for k in range(2):
            low_ref[k, at, :] = value[:, k * COLS : k * COLS + COLS]

    settle(14)
    for i in range(2):
        for copy in gathers[i]:
            copy.wait_recv()
        place = panel.at[core, i]
        handed = send(place, place, p3_s.at[i], p3_r.at[i], sibling)
        low_rank_piece(core, i)
        if i == 1:
            settle(1)
        handed.wait_recv()
        low_rank_piece(1 - core, i)
    settle()


def last_kernel(low_ref, values_ref, bounds_ref, low_rank_ref, sparse_ref):
    bound = bounds_ref[...]
    low_rank = low_ref[...]
    gap = values_ref[...] - low_rank
    low_rank_ref[...] = low_rank
    sparse_ref[...] = gap - jnp.minimum(jnp.maximum(gap, -bound), bound)


def on_device(series_values, previous_sparse, row_picks, tick_picks, sketch, thresholds):
    vmem = pl.BlockSpec(memory_space=pltpu.VMEM)
    hbm = pl.BlockSpec(memory_space=pltpu.HBM)
    dma = pltpu.SemaphoreType.DMA
    low, values, bounds = pl.pallas_call(
        main_kernel,
        out_shape=(
            jax.ShapeDtypeStruct((2, HALF, COLS), F32),
            jax.ShapeDtypeStruct((ROWS, COLS), F32),
            jax.ShapeDtypeStruct((1, COLS), F32),
        ),
        in_specs=[hbm] * 6,
        out_specs=(vmem,) * 3,
        scratch_shapes=[
            pltpu.VMEM((ROWS, COLS), F32),
            pltpu.VMEM((16, 128), jnp.int32),
            pltpu.VMEM((PICKS // 128, 128), jnp.int32),
            pltpu.VMEM((RANK, PICKS), F32),
            pltpu.VMEM((16, 128), F32),
            pltpu.VMEM((16, 128), F32),
            pltpu.VMEM((CAP, 128), jnp.int32),
            pltpu.VMEM((HALF, 2 * COLS), BF16),
            pltpu.VMEM((HALF, 2 * COLS), BF16),
            pltpu.VMEM((CAP, COLS), F32),
            pltpu.VMEM((2, RANK, 128), F32),
            pltpu.VMEM((RANK, 128), F32),
            pltpu.VMEM((RANK, 128), F32),
            pltpu.VMEM((8, RANK, 128), F32),
            pltpu.VMEM((128, COLS), F32),
            pltpu.VMEM((2, 4, 16, COLS), F32),
            pltpu.VMEM((2, 8, 16, COLS), F32),
            pltpu.VMEM((16, COLS), F32),
            pltpu.VMEM((4, 16, COLS), F32),
            pltpu.VMEM((4, 16, COLS), F32),
            pltpu.VMEM((2, 8, 32, 128), F32),
            pltpu.VMEM((2, 8, 32, 128), F32),
            pltpu.VMEM((2, 8, 32, 128), F32),
            pltpu.VMEM((2, 8, 32, 128), F32),
            pltpu.VMEM((2, 2, 8, 32, 128), F32),
            pltpu.VMEM((2, 16, 128), F32),
            pltpu.VMEM((16, 128), F32),
            pltpu.VMEM((16, 128), F32),
            pltpu.VMEM((8, 16, 128), F32),
            pltpu.VMEM((2, 16, 128), F32),
            dma((8,)),
            dma((2,)), dma((2,)), dma((8,)), dma((8,)),
            dma((2, 4)), dma((2, 8)), dma((4,)), dma((4,)), dma((8,)), dma((4,)),
            dma((2,)), dma((2,)), dma((2, 8)), dma((2, 8)), dma((2, 8)), dma((2, 8)),
            dma((2,)), dma((2,)),
            dma((8,)), dma((8,)), dma((2,)), dma((2,)),
        ],
        compiler_params=pltpu.CompilerParams(
            collective_id=0, has_side_effects=True, vmem_limit_bytes=24 << 20
        ),
        name="cur_core",
    )(
        *(
            pltpu.with_memory_space_constraint(x, pltpu.HBM)
            for x in (
                series_values,
                previous_sparse,
                row_picks.reshape(16, 128),
                tick_picks.reshape(PICKS // 128, 128),
                sketch.T,
                thresholds.reshape(1, COLS),
            )
        )
    )
    steps = 2
    block = pl.BlockSpec((ROWS // steps, COLS), lambda i: (i, 0))
    return pl.pallas_call(
        last_kernel,
        grid=(steps,),
        out_shape=(jax.ShapeDtypeStruct((ROWS, COLS), F32),) * 2,
        in_specs=[block, block, pl.BlockSpec((1, COLS), lambda i: (0, 0))],
        out_specs=(block, block),
        compiler_params=pltpu.CompilerParams(vmem_limit_bytes=16 << 20),
        name="low_rank_and_sparse",
    )(low.reshape(ROWS, COLS), values, bounds)


def solution(mesh):
    placed = (P("series", "tick"), P("series", "tick"), P(), P(), P(), P("tick"))
    return jax.shard_map(
        on_device,
        mesh=mesh,
        in_specs=placed,
        out_specs=(P("series", "tick"), P("series", "tick")),
        check_vma=False,
    )
```
